32 devices in a mesh: groups: 2 (over y), batch: 16 (over z, x, core).
Axes of the slice: x: 2, y: 2, z: 4, core: 2. Of those that a mesh axis runs over, the one named last changes fastest.
Arguments:
- tokens: bfloat16 [96, 6144], P(('groups', 'batch')), parts along dimension 0, may hold values from -6 to 6
- w_proj: bfloat16 [6144, 16384], P(None, 'batch'), may hold values from -0.078125 to 0.078125
- w_out: bfloat16 [4096, 6144], P(None, 'batch'), may hold values from -0.09375 to 0.09375
- decay_rate: float32 [32], replicated, may hold values from 0.02 to 2
- norm_gain: float32 [4096], replicated, may hold values from 0.1 to 1.9
- cache_tiles: bfloat16 [5376, 128, 128], P(('groups', 'batch')), parts along dimension 0, may hold values from -6 to 6
- tile_scales: float32 [5376], P(('groups', 'batch')), parts along dimension 0, may hold values from 0.1 to 1
- tile_holder: int32 [96, 32], P(('groups', 'batch')), parts along dimension 0, may hold values from 0 to 15, as said below
- tile_rank: int32 [96, 32], P(('groups', 'batch')), parts along dimension 0, may hold values from 0 to 11, as said below
- send_slot: int32 [32, 16, 12], P(('groups', 'batch')), parts along dimension 0, may hold values from -1 to 167, as said below
Outputs:
- mixed_out: bfloat16 [96, 6144], P('groups', 'batch'), parts along dimension 0
- new_cache: bfloat16 [5376, 128, 128], P(('groups', 'batch')), parts along dimension 0
The draws below stay inside these ranges and needn't reach their ends.
There are 2 independent parts, one for each index of `groups`. The reference program is written for one: setup_inputs(seed, part) draws one part's arguments, and reference() takes and returns one part's arrays. A program takes and returns all parts, laid end to end along the dimension named above; an argument that names none is the same for every part. Nothing has to cross between parts.
Inputs may be any that keep to these rules, and one draw needn't show every extreme that they name: tile_holder[s, h] is the device along batch whose slots hold the tile of session s and head h; a holder holds up to 168 tiles, and some holders hold that many. tile_rank[s, h] is the tile's position among the tiles that its holder sends to the owner of s (device s // 3); some holder sends 12 tiles to some owner in every draw. send_slot[p, o, r] is the slot in holder p of the tile at position r that p sends to owner o, -1 where p sends fewer than r + 1 tiles to o; it agrees with tile_holder and tile_rank, names every tile of every session once and names no slot twice.
All inputs are finite; a program needn't handle non-finite values.
Results may differ from the reference program's by a relative error of at most 0.0085.
Values may be sent and summed in bfloat16 or wider, within the bound.
No kernel may reach another device: no remote copies, remote signals or barrier semaphores. Data moves between devices by JAX's collectives and lax.ppermute only.
A program may use at most 128 MiB of HBM per device.

```python
import math
import jax
import jax.numpy as jnp
from jax import lax

D = 6144
HEADS = 32
HEAD_DIM = 128
SES_DEV = 3
SESSIONS = 48
SLOTS = 168
CAP = 12
N_BATCH = 16


def permute_one(key_item, length):
    return jax.random.permutation(key_item, length).astype(jnp.int32)


def layout(key):
    tile_count = SES_DEV * HEADS
    pair_count = tile_count // 2
    devices = N_BATCH
    pattern = jnp.array([7, 7, 3, 3, 3, 3, 3, 3], dtype=jnp.int32)
    loads = jnp.tile(pattern, devices // 8) * (tile_count // 8)
    loads = loads[jax.random.permutation(jax.random.fold_in(key, 11), devices)]
    ends = jnp.cumsum(loads).astype(jnp.int32)
    starts = ends - loads
    positions = jnp.arange(devices * pair_count, dtype=jnp.int32)
    holders = jnp.sum((positions[:, None] >= ends[None, :]).astype(jnp.int32), axis=1).astype(jnp.int32)
    within = positions - starts[holders]
    pair_rank = within // devices
    owners = positions % devices
    pair_index = positions // devices
    slot_keys = jax.random.split(jax.random.fold_in(key, 12), devices)
    slot_perm = jax.vmap(lambda key_item: permute_one(key_item, SLOTS))(slot_keys)
    tile_keys = jax.random.split(jax.random.fold_in(key, 13), devices)
    tile_perm = jax.vmap(lambda key_item: permute_one(key_item, tile_count))(tile_keys)
    holder_table = jnp.zeros((SESSIONS, HEADS), jnp.int32)
    rank_table = jnp.zeros((SESSIONS, HEADS), jnp.int32)
    slot_table = jnp.full((devices, devices, CAP), -1, jnp.int32)
    for member in range(2):
        tile_ids = tile_perm[owners, 2 * pair_index + member]
        sessions = owners * SES_DEV + tile_ids // HEADS
        head_ids = tile_ids % HEADS
        ranks = 2 * pair_rank + member
        slots = slot_perm[holders, 2 * within + member]
        holder_table = holder_table.at[sessions, head_ids].set(holders)
        rank_table = rank_table.at[sessions, head_ids].set(ranks)
        slot_table = slot_table.at[holders, owners, ranks].set(slots)
    return (holder_table, rank_table, slot_table)


def draw_tile_holder(key, part):
    return layout(key)[0]


def draw_tile_rank(key, part):
    return layout(key)[1]


def draw_send_slot(key, part):
    return layout(key)[2]


def shard_levels(key, dims, shards, low, top_value):
    loudness = 1.0
    for position, shards_of in shards:
        steps = jax.random.uniform(jax.random.fold_in(jax.random.fold_in(key, 6), position), (shards_of,), jnp.float32, low / len(shards), top_value / len(shards))
        loudness = loudness * jnp.repeat(jnp.exp(steps), dims[position] // shards_of).reshape((-1,) + (1,) * (len(dims) - 1 - position))
    return loudness


def scatter_about(rng, extent, spread, limit, shards=(), kind=jnp.bfloat16):
    drawn = jax.random.normal(rng, extent, jnp.float32) * spread
    if len(shards) > 0:
        drawn = shard_levels(rng, extent, shards, -0.22, 0.18) * drawn
    return jnp.clip(drawn, min=-limit, max=limit).astype(kind)


def setup_inputs(seed: int = 0, part: int = 0) -> dict:
    key_list = jax.random.split(jax.random.key(seed), 11)
    part_splits = jax.random.split(jax.random.fold_in(key_list[10], part), 11)
    tokens = scatter_about(part_splits[0], (SESSIONS, D), 1.0, 6.0, ((0, 16),))
    w_proj = scatter_about(key_list[1], (D, 4 * HEADS * HEAD_DIM), D ** -0.5, 0.078125, ((1, 16),))
    w_out = scatter_about(key_list[2], (HEADS * HEAD_DIM, D), (HEADS * HEAD_DIM) ** -0.5, 0.09375, ((1, 16),))
    decay_rate = jnp.clip(jnp.exp(jax.random.uniform(key_list[3], (HEADS,), jnp.float32, math.log(0.02), math.log(2.0))), 0.02, 2.0)
    norm_gain = jnp.clip(1.0 + 0.18 * jax.random.normal(key_list[4], (HEADS * HEAD_DIM,), jnp.float32), 0.1, 1.9)
    cache_tiles = scatter_about(part_splits[5], (N_BATCH * SLOTS, HEAD_DIM, HEAD_DIM), 1.0, 6.0, ((0, 16),))
    tile_scales = jnp.clip(jnp.exp(math.log(1.0) - 2.3025851 * jax.random.uniform(part_splits[6], (N_BATCH * SLOTS,), jnp.float32) ** shard_levels(part_splits[6], (N_BATCH * SLOTS,), ((0, 16),), -0.2, 0.2)), 0.1, 1.0)
    tile_holder = draw_tile_holder(jax.random.fold_in(jax.random.fold_in(key_list[10], part), 71), part)
    tile_rank = draw_tile_rank(jax.random.fold_in(jax.random.fold_in(key_list[10], part), 71), part)
    send_slot = draw_send_slot(jax.random.fold_in(jax.random.fold_in(key_list[10], part), 71), part)
    return {"tokens": tokens, "w_proj": w_proj, "w_out": w_out, "decay_rate": decay_rate, "norm_gain": norm_gain, "cache_tiles": cache_tiles, "tile_scales": tile_scales, "tile_holder": tile_holder, "tile_rank": tile_rank, "send_slot": send_slot}


def advance(tile_rows, scale_rows, factor, queries, key_rows, values):
    tile_scale = scale_rows[:, None, None]
    states = factor[:, None, None] * (tile_rows.astype(jnp.float32) * tile_scale)
    states = states + key_rows.astype(jnp.float32)[:, :, None] * values.astype(jnp.float32)[:, None, :]
    readout = jnp.einsum('ti,tij->tj', queries.astype(jnp.float32), states, precision=lax.Precision.HIGHEST)
    fresh_tiles = (states / tile_scale).astype(jnp.bfloat16)
    return (readout, fresh_tiles)

def reference(tokens, w_proj, w_out, decay_rate, norm_gain, cache_tiles, tile_scales, tile_holder, tile_rank, send_slot):
    inner_width = HEADS * HEAD_DIM
    projected = jnp.dot(tokens, w_proj, preferred_element_type=jnp.float32)
    activated = jnp.concatenate([jax.nn.silu(projected[:, :3 * inner_width]), jax.nn.sigmoid(projected[:, 3 * inner_width:])], axis=1).astype(jnp.bfloat16)
    owners = (jnp.arange(SESSIONS, dtype=jnp.int32) // SES_DEV).astype(jnp.int32)
    owner_grid = jnp.broadcast_to(owners[:, None], (SESSIONS, HEADS))
    slots = send_slot[tile_holder, owner_grid, tile_rank].astype(jnp.int32)
    places = (tile_holder * SLOTS + slots).astype(jnp.int32)
    factor = jnp.exp(-decay_rate.astype(jnp.float32))

    def session_step(inputs):
        session_row, place_row = inputs
        queries = session_row[:inner_width].reshape(HEADS, HEAD_DIM)
        key_rows = session_row[inner_width:2 * inner_width].reshape(HEADS, HEAD_DIM)
        values = session_row[2 * inner_width:3 * inner_width].reshape(HEADS, HEAD_DIM)
        readout, fresh_tiles = advance(cache_tiles[place_row], tile_scales[place_row], factor, queries, key_rows, values)
        return (readout.reshape(inner_width), fresh_tiles)
    readout, fresh_tiles = lax.map(session_step, (activated, places))
    squares = lax.optimization_barrier(jnp.mean(readout * readout, axis=1, keepdims=True))
    gate_values = activated[:, 3 * inner_width:].astype(jnp.float32)
    hidden = (readout * lax.rsqrt(squares + 1e-06) * norm_gain * gate_values).astype(jnp.bfloat16)
    mixed_out = jnp.dot(hidden, w_out, preferred_element_type=jnp.float32).astype(jnp.bfloat16)
    new_cache = cache_tiles.at[places.reshape(-1)].set(fresh_tiles.reshape(-1, HEAD_DIM, HEAD_DIM))
    return (mixed_out, new_cache)
```

```python
import functools

import jax
import jax.numpy as jnp
from jax import lax
from jax.experimental import pallas as pl
from jax.experimental.pallas import tpu as pltpu
from jax.sharding import PartitionSpec as P

VMEM_LIMIT = 60 * 1024 * 1024
BF16 = jnp.bfloat16
F32 = jnp.float32


def block_order(devices):
    order, bit = [0], devices // 2
    while bit >= 1:
        order = order + [o ^ bit for o in order]
        bit //= 2
    return order


def gather_blocks(block, devices):
    held = block[None]
    bit = devices // 2
    while bit >= 1:
        got = lax.ppermute(held, "batch", [(i, i ^ bit) for i in range(devices)])
        held = jnp.concatenate([held, got], axis=0)
        bit //= 2
    return held


def project_kernel(
    chunk, inner_width, flag_ref, source_ref, x_ref, w_ref, act_ref, index_ref, rows, wbuf, sems
):
    devices, _, width = x_ref.shape
    sessions = act_ref.shape[0]
    own = sessions // devices
    steps = width // chunk
    copies = []
    for step in range(steps):
        part = pl.ds(step * chunk, chunk)
        copies.append(pltpu.make_async_copy(w_ref.at[part], wbuf.at[part], sems.at[step]))
        copies[-1].start()
    indices = []
    for j in range(devices):
        block = x_ref[j].astype(F32)
        rows[j * own : (j + 1) * own, :] = block[:own]
        for i in range(own):
            indices.append(block[own : own + 1, i * 128 : (i + 1) * 128])
    total = jnp.zeros(act_ref.shape, F32)
    for step in range(steps):
        copies[step].wait()
        part = slice(step * chunk, (step + 1) * chunk)
        total += jnp.dot(
            rows[:, part].astype(BF16), wbuf[part, :], preferred_element_type=F32
        )
    gate = jax.nn.sigmoid(total)
    active = jnp.where(flag_ref[0] > 0, gate, total * gate).astype(BF16)
    place = (
        lax.broadcasted_iota(jnp.int32, (sessions, sessions), 1) == source_ref[...]
    ).astype(F32).astype(BF16)
    act_ref[...] = jnp.dot(place, active, preferred_element_type=F32).astype(BF16)
    table = jnp.concatenate(indices, axis=0).astype(BF16)
    index_ref[...] = jnp.dot(place, table, preferred_element_type=F32).astype(jnp.int32)


def project(x, w, flag, source, inner_width):
    devices, _, width = x.shape
    sessions = source.shape[0]
    cols = w.shape[1]
    chunk = width // 8
    return pl.pallas_call(
        functools.partial(project_kernel, chunk, inner_width),
        out_shape=(
            jax.ShapeDtypeStruct((sessions, cols), BF16),
            jax.ShapeDtypeStruct((sessions, 128), jnp.int32),
        ),
        in_specs=[
            pl.BlockSpec(memory_space=pltpu.SMEM),
            pl.BlockSpec(memory_space=pltpu.VMEM),
            pl.BlockSpec(memory_space=pltpu.VMEM),
            pl.BlockSpec(memory_space=pl.ANY),
        ],
        out_specs=(
            pl.BlockSpec(memory_space=pltpu.VMEM),
            pl.BlockSpec(memory_space=pltpu.VMEM),
        ),
        scratch_shapes=[
            pltpu.VMEM((sessions, width), F32),
            pltpu.VMEM(w.shape, BF16),
            pltpu.SemaphoreType.DMA((width // chunk,)),
        ],
        compiler_params=pltpu.CompilerParams(vmem_limit_bytes=VMEM_LIMIT),
        cost_estimate=pl.CostEstimate(
            flops=2 * sessions * width * cols, bytes_accessed=2 * width * cols, transcendentals=0
        ),
        name="project",
    )(flag, source, x, w)


def readout_kernel(
    heads,
    order_ref,
    slot_ref,
    row_ref,
    head_ref,
    decay_ref,
    scale_ref,
    act_ref,
    cache_ref,
    out_ref,
    key_ref,
    value_ref,
    flat,
    tiles,
    query,
    sems,
):
    devices, sessions, cols = act_ref.shape
    per = cols // 128
    pieces = sems.shape[0]
    step = cache_ref.shape[0] // pieces
    copies = []
    for piece in range(pieces):
        part = pl.ds(piece * step, step)
        copies.append(pltpu.make_async_copy(cache_ref.at[part], tiles.at[part], sems.at[piece]))
        copies[-1].start()
    rows_each = per * sessions

    def place(j):
        device = order_ref[j]

        @pl.when(device < 3 * devices // 4)
        def _():
            base = pl.multiple_of(device * rows_each, 8)
            for b in range(per):
                flat[pl.ds(base + b * sessions, sessions), :] = act_ref[
                    j, :, b * 128 : (b + 1) * 128
                ].astype(F32)

    if devices <= 16:
        for j in range(devices):
            place(j)
    else:
        pl.loop(0, devices)(place)
    entries = out_ref.shape[0]
    comp = heads * sessions

    @pl.loop(0, entries // 8)
    def _(group):
        for u in range(8):
            e = group * 8 + u
            row = row_ref[e]
            query[pl.ds(e, 1), :] = flat[pl.ds(row, 1), :]
            key_ref[pl.ds(e, 1), :] = flat[pl.ds(row + comp, 1), :]
            value_ref[pl.ds(e, 1), :] = flat[pl.ds(row + 2 * comp, 1), :]

    for copy in copies:
        copy.wait()

    @pl.loop(0, entries // 8)
    def _(group):
        base = pl.multiple_of(group * 8, 8)
        q8 = query[pl.ds(base, 8), :]
        outs = []
        for u in range(8):
            e = base + u
            slot = jnp.maximum(slot_ref[e], 0)
            factor = decay_ref[head_ref[e]] * scale_ref[slot]
            prod = jnp.dot(
                q8[u : u + 1].astype(BF16), tiles[slot], preferred_element_type=F32
            )
            outs.append(prod * factor)
        near = jnp.sum(q8 * key_ref[pl.ds(base, 8), :], axis=1, keepdims=True)
        query[pl.ds(base, 8), :] = (
            jnp.concatenate(outs, axis=0) + near * value_ref[pl.ds(base, 8), :]
        )

    out_ref[...] = query[...].astype(BF16)


def read_states(act, cache, order, slot, row, head, decay, scale, heads):
    entries = slot.shape[0]
    devices, sessions, cols = act.shape
    smem = pl.BlockSpec(memory_space=pltpu.SMEM)
    vmem = pl.BlockSpec(memory_space=pltpu.VMEM)
    return pl.pallas_call(
        functools.partial(readout_kernel, heads),
        out_shape=(
            jax.ShapeDtypeStruct((entries, 128), BF16),
            jax.ShapeDtypeStruct((entries, 128), F32),
            jax.ShapeDtypeStruct((entries, 128), F32),
        ),
        in_specs=[smem] * 6 + [vmem, pl.BlockSpec(memory_space=pl.ANY)],
        out_specs=(vmem, vmem, vmem),
        scratch_shapes=[
            pltpu.VMEM((3 * heads * sessions, 128), F32),
            pltpu.VMEM(cache.shape, BF16),
            pltpu.VMEM((entries, 128), F32),
            pltpu.SemaphoreType.DMA((8,)),
        ],
        compiler_params=pltpu.CompilerParams(vmem_limit_bytes=VMEM_LIMIT),
        cost_estimate=pl.CostEstimate(
            flops=2 * entries * 128 * 128, bytes_accessed=2 * cache.size, transcendentals=0
        ),
        name="readout",
    )(order, slot, row, head, decay, scale, act, cache)


def update_kernel(
    slot_ref, head_ref, decay_ref, inverse_ref, key_ref, value_ref, cache_ref, out_ref
):
    @pl.loop(0, cache_ref.shape[0] // 8)
    def _(group):
        base = group * 8
        out_ref[pl.ds(base, 8)] = cache_ref[pl.ds(base, 8)]

    @pl.loop(0, slot_ref.shape[0] // 8)
    def _(group):
        base = pl.multiple_of(group * 8, 8)
        keys = key_ref[pl.ds(base, 8), :].astype(BF16)
        values = value_ref[pl.ds(base, 8), :].astype(BF16)
        for u in range(8):
            slot = slot_ref[base + u]

            @pl.when(slot >= 0)
            def _():
                outer = lax.dot_general(
                    keys[u : u + 1],
                    values[u : u + 1],
                    (((0,), (0,)), ((), ())),
                    preferred_element_type=F32,
                )
                fresh = decay_ref[head_ref[base + u]] * cache_ref[slot].astype(F32)
                out_ref[slot] = (fresh + outer * inverse_ref[slot]).astype(BF16)


def update_tiles(cache, key_rows, values, slot, head, decay, inverse):
    smem = pl.BlockSpec(memory_space=pltpu.SMEM)
    vmem = pl.BlockSpec(memory_space=pltpu.VMEM)
    return pl.pallas_call(
        update_kernel,
        out_shape=jax.ShapeDtypeStruct(cache.shape, BF16),
        in_specs=[smem] * 4 + [vmem] * 3,
        out_specs=vmem,
        compiler_params=pltpu.CompilerParams(vmem_limit_bytes=VMEM_LIMIT),
        cost_estimate=pl.CostEstimate(
            flops=4 * cache.size, bytes_accessed=4 * cache.size, transcendentals=0
        ),
        name="update",
    )(slot, head, decay, inverse, key_rows, values, cache)


def finish_kernel(
    order_ref, pick_ref, read_ref, act_ref, gain_ref, w_ref, out_ref, flat, hidden, merged
):
    devices, entries, _ = read_ref.shape
    sessions = act_ref.shape[1]
    per = act_ref.shape[2] // 128
    heads = merged.shape[1] // 128
    first = 3 * devices // 4

    def place(j):
        device = order_ref[j]
        base = pl.multiple_of(device * entries, 8)
        flat[pl.ds(base, entries), :] = read_ref[j].astype(F32)

    if devices <= 16:
        for j in range(devices):
            place(j)
    else:
        pl.loop(0, devices)(place)

    @pl.loop(0, heads * sessions // 16)
    def _(group):
        for u in range(16):
            e = group * 16 + u
            hidden[pl.ds(e, 1), :] = flat[pl.ds(pick_ref[e], 1), :]

    squares = jnp.zeros((sessions, 128), F32)
    for h in range(heads):
        block = hidden[h * sessions : (h + 1) * sessions, :]
        squares += block * block
    mean = jnp.sum(squares, axis=1, keepdims=True) * (1.0 / (heads * 128))
    norm = lax.rsqrt(mean + 1e-6)
    for h in range(heads):
        block = hidden[h * sessions : (h + 1) * sessions, :]
        device = first + h // per
        gate = act_ref[order_ref[devices + device], :, (h % per) * 128 : (h % per + 1) * 128]
        block = block * norm * gain_ref[h : h + 1, :] * gate.astype(F32)
        merged[:, h * 128 : (h + 1) * 128] = block.astype(BF16)
    out_ref[...] = jnp.dot(merged[...], w_ref[...], preferred_element_type=F32).astype(BF16)


def finish(read, act, order, pick, gain, w_out):
    devices, entries, _ = read.shape
    sessions = act.shape[1]
    width = w_out.shape[0]
    smem = pl.BlockSpec(memory_space=pltpu.SMEM)
    vmem = pl.BlockSpec(memory_space=pltpu.VMEM)
    return pl.pallas_call(
        finish_kernel,
        out_shape=jax.ShapeDtypeStruct((sessions, w_out.shape[1]), BF16),
        in_specs=[smem] * 2 + [vmem] * 4,
        out_specs=vmem,
        scratch_shapes=[
            pltpu.VMEM((devices * entries, 128), F32),
            pltpu.VMEM((sessions * width // 128, 128), F32),
            pltpu.VMEM((sessions, width), BF16),
        ],
        compiler_params=pltpu.CompilerParams(vmem_limit_bytes=VMEM_LIMIT),
        cost_estimate=pl.CostEstimate(
            flops=2 * sessions * w_out.size, bytes_accessed=2 * w_out.size, transcendentals=0
        ),
        name="finish",
    )(order, pick, read, act, gain, w_out)


def on_device(
    tokens,
    w_proj,
    w_out,
    decay_rate,
    norm_gain,
    cache_tiles,
    tile_scales,
    tile_holder,
    tile_rank,
    send_slot,
):
    devices = lax.axis_size("batch")
    me = lax.axis_index("batch")
    heads = decay_rate.shape[0]
    inner_width = heads * cache_tiles.shape[-1]
    own, width = tokens.shape
    sessions = own * devices
    capacity = send_slot.shape[-1]
    cols = w_proj.shape[1]

    relative = jnp.array(block_order(devices), jnp.int32)
    inverse_order = [0] * devices
    for j, o in enumerate(block_order(devices)):
        inverse_order[o] = j
    bits = devices.bit_length() - 1
    owners = jnp.arange(devices, dtype=jnp.int32)
    crossed = owners ^ me
    position = sum(((crossed >> k) & 1) << (bits - 1 - k) for k in range(bits))
    order = jnp.concatenate([relative ^ me, position])
    source = (position[:, None] * own + jnp.arange(own, dtype=jnp.int32)[None]).reshape(sessions, 1)
    flag = (me * cols >= 3 * inner_width).astype(jnp.int32).reshape(1)

    table = jnp.concatenate([tile_holder, tile_rank], axis=1).astype(BF16)
    table = jnp.pad(table, ((0, 0), (0, 128 - 2 * heads))).reshape(1, own * 128)
    table = jnp.pad(table, ((0, 0), (0, width - own * 128)))
    sent = jnp.concatenate([tokens, table], axis=0)

    blocks = gather_blocks(sent, devices)
    act, index = project(blocks, w_proj, flag, source, inner_width)
    all_act = gather_blocks(act, devices)

    holder = index[:, :heads]
    rank = index[:, heads : 2 * heads]
    owner = jnp.arange(sessions, dtype=jnp.int32)[:, None] // own
    pick = ((holder * devices + owner) * capacity + rank).T.reshape(-1)
    local = (
        jnp.arange(heads, dtype=jnp.int32)[None, :] * own
        + jnp.arange(own, dtype=jnp.int32)[:, None]
    ).reshape(-1)
    mine = jnp.where(holder == me, rank, -1).reshape(devices, own * heads)
    ranks = jnp.arange(capacity, dtype=jnp.int32)
    found = jnp.sum(
        jnp.where(mine[:, None, :] == ranks[None, :, None], local[None, None, :], 0), axis=2
    )
    head = found // own
    session = found % own + own * jnp.arange(devices, dtype=jnp.int32)[:, None]
    row = (head * sessions + session).reshape(-1)
    head = head.reshape(-1)
    slot = send_slot.reshape(-1)
    decay = jnp.exp(-decay_rate)

    read, key_rows, values = read_states(
        all_act, cache_tiles, order, slot, row, head, decay, tile_scales, heads
    )
    all_read = gather_blocks(read, devices)
    new_cache = update_tiles(
        cache_tiles, key_rows, values, slot, head, decay, 1.0 / tile_scales
    )
    mixed_out = finish(all_read, all_act, order, pick, norm_gain.reshape(heads, 128), w_out)
    return (mixed_out, new_cache)


def solution(mesh):
    return jax.shard_map(
        on_device,
        mesh=mesh,
        in_specs=(
            P(("groups", "batch"), None),
            P(None, "batch"),
            P(None, "batch"),
            P(),
            P(),
            P(("groups", "batch"), None, None),
            P(("groups", "batch")),
            P(("groups", "batch"), None),
            P(("groups", "batch"), None),
            P(("groups", "batch"), None, None),
        ),
        out_specs=(P("groups", "batch"), P(("groups", "batch"), None, None)),
        check_vma=False,
    )
```

```python
import functools

import jax
import jax.numpy as jnp
from jax import lax
from jax.experimental import pallas as pl
from jax.experimental.pallas import tpu as pltpu
from jax.sharding import PartitionSpec as P

VMEM_LIMIT = 60 * 1024 * 1024
BF16 = jnp.bfloat16
F32 = jnp.float32
I32 = jnp.int32
SMEM = pl.BlockSpec(memory_space=pltpu.SMEM)
VMEM = pl.BlockSpec(memory_space=pltpu.VMEM)
ANY = pl.BlockSpec(memory_space=pl.ANY)


def block_order(devices):
    order, bit = [0], devices // 2
    while bit >= 1:
        order = order + [o ^ bit for o in order]
        bit //= 2
    return order


def gather_pieces(block, devices):
    held, bit = [block], devices // 2
    while bit >= 1:
        pairs = [(i, i ^ bit) for i in range(devices)]
        held = held + [lax.ppermute(piece, "batch", pairs) for piece in held]
        bit //= 2
    return held


def pack_kernel(heads, tokens_ref, holder_ref, rank_ref, out_ref):
    own, width = tokens_ref.shape
    parts = []
    for i in range(own):
        parts.append(holder_ref[i : i + 1, :].astype(F32))
        parts.append(rank_ref[i : i + 1, :].astype(F32))
        parts.append(jnp.zeros((1, 128 - 2 * heads), F32))
    parts.append(jnp.zeros((1, width - own * 128), F32))
    table = jnp.concatenate(parts, axis=1)
    block = jnp.concatenate([tokens_ref[...].astype(F32), table], axis=0)
    out_ref[...] = block.astype(BF16)


def pack(tokens, holder, rank):
    own, width = tokens.shape
    return pl.pallas_call(
        functools.partial(pack_kernel, holder.shape[1]),
        out_shape=jax.ShapeDtypeStruct((own + 1, width), BF16),
        in_specs=[VMEM] * 3,
        out_specs=VMEM,
        name="pack",
    )(tokens, holder, rank)


def project_kernel(devices, heads, slots, steps, *refs):
    me_ref, send_ref, w_ref = refs[:3]
    pieces = refs[3 : 3 + devices]
    act_ref, pick_ref, slot_ref, rows, wbuf, sems = refs[3 + devices :]
    order = block_order(devices)
    bits = devices.bit_length() - 1
    sessions, cols = act_ref.shape
    own = sessions // devices
    capacity = send_ref.shape[1]
    width = w_ref.shape[0]
    chunk = width // steps
    me = me_ref[0]
    copies = []
    for step in range(steps):
        part = pl.ds(step * chunk, chunk)
        copies.append(pltpu.make_async_copy(w_ref.at[part], wbuf.at[part], sems.at[step]))
        copies[-1].start()

    lane = lax.broadcasted_iota(I32, (1, sessions), 1)
    target = jnp.zeros((1, sessions), I32)
    source = jnp.zeros((1, sessions), I32)
    indices = []
    for j in range(devices):
        block = pieces[j][...].astype(F32)
        rows[j * own : (j + 1) * own, :] = block[:own]
        for i in range(own):
            indices.append(block[own : own + 1, i * 128 : (i + 1) * 128])
        inside = (lane >= j * own) & (lane < (j + 1) * own)
        target = jnp.where(inside, lane + ((me ^ order[j]) - j) * own, target)
        crossed = me ^ j
        position = jnp.int32(0)
        for k in range(bits):
            position = position + (((crossed >> k) & 1) << (bits - 1 - k))
        source = jnp.where(inside, lane + (position - j) * own, source)
    grid_row = lax.broadcasted_iota(I32, (sessions, sessions), 0)
    place = (grid_row == target).astype(F32).astype(BF16)
    place_t = (grid_row == source).astype(F32).astype(BF16)

    table = jnp.concatenate(indices, axis=0)
    table = jnp.dot(table.T.astype(BF16), place_t, preferred_element_type=F32).astype(I32)
    holder = table[:heads]
    rank = table[heads : 2 * heads]
    owner = (lane * (65536 // own + 1)) >> 16
    pick_ref[...] = (holder * devices + owner) * capacity + rank

    owner_row = lax.broadcasted_iota(I32, (devices, sessions), 0)
    spread = (owner_row == owner).astype(F32).astype(BF16)
    sent = send_ref[...].astype(F32).T.astype(BF16)
    sent = jnp.dot(sent, spread, preferred_element_type=F32).astype(I32)
    slot = jnp.full((heads, sessions), -1, I32)
    for r in range(capacity):
        slot = jnp.where(rank == r, sent[r : r + 1, :], slot)
    slot = jnp.where(holder == me, slot, -1)
    entry = owner * capacity + rank
    padded = slot_ref.shape[1]
    slot_lane = lax.broadcasted_iota(I32, (heads, padded), 1)
    head_row = lax.broadcasted_iota(I32, (heads, padded), 0)
    found = jnp.zeros((heads, padded), I32)
    found_entry = jnp.zeros((heads, padded), I32)
    for s in range(sessions):
        same = slot[:, s : s + 1] == slot_lane
        found = jnp.where(same, head_row * sessions + (s + 1), found)
        found_entry = jnp.where(same, entry[:, s : s + 1], found_entry)
    code = jnp.sum(found.astype(F32), axis=0, keepdims=True).astype(I32) - 1
    code_entry = jnp.sum(found_entry.astype(F32), axis=0, keepdims=True).astype(I32)
    used = code >= 0
    head = jnp.sum((found > 0).astype(F32) * head_row.astype(F32), axis=0, keepdims=True)
    slot_ref[0:1, :] = jnp.where(used, code, 3 * heads * sessions)
    slot_ref[1:2, :] = jnp.where(used, head.astype(I32), -1)
    slot_ref[2:3, :] = jnp.where(used, code_entry, devices * capacity)
    slot_ref[3:8, :] = jnp.zeros((5, padded), I32)

    total = jnp.zeros(act_ref.shape, F32)
    for step in range(steps):
        copies[step].wait()
        part = slice(step * chunk, (step + 1) * chunk)
        total += jnp.dot(rows[:, part].astype(BF16), wbuf[part, :], preferred_element_type=F32)
    gate = jax.nn.sigmoid(total)
    is_gate = me * cols >= 3 * heads * 128
    active = jnp.where(is_gate, gate, total * gate).astype(BF16)
    act_ref[...] = jnp.dot(place, active, preferred_element_type=F32).astype(BF16)


def project(pieces, w, me, send, heads, slots):
    devices = len(pieces)
    own = pieces[0].shape[0] - 1
    sessions = own * devices
    width, cols = w.shape
    steps = 8
    padded = (slots + 127) // 128 * 128
    return pl.pallas_call(
        functools.partial(project_kernel, devices, heads, slots, steps),
        out_shape=(
            jax.ShapeDtypeStruct((sessions, cols), BF16),
            jax.ShapeDtypeStruct((heads, sessions), I32),
            jax.ShapeDtypeStruct((8, padded), I32),
        ),
        in_specs=[SMEM, VMEM, ANY] + [VMEM] * devices,
        out_specs=(VMEM, VMEM, VMEM),
        scratch_shapes=[
            pltpu.VMEM((sessions, width), F32),
            pltpu.VMEM(w.shape, BF16),
            pltpu.SemaphoreType.DMA((steps,)),
        ],
        compiler_params=pltpu.CompilerParams(vmem_limit_bytes=VMEM_LIMIT),
        cost_estimate=pl.CostEstimate(
            flops=2 * sessions * width * cols, bytes_accessed=2 * width * cols, transcendentals=0
        ),
        name="project",
    )(me, send, w, *pieces)


def advance_kernel(devices, heads, chunks, *refs):
    me_ref, slot_ref, rate_ref, scale_ref, cache_ref = refs[:5]
    pieces = refs[5 : 5 + devices]
    (read_ref, gate_ref, out_ref, flat, tiles, fresh, query, keys, values, reads, in_sems, out_sems) = refs[
        5 + devices :
    ]
    order = block_order(devices)
    sessions, cols = pieces[0].shape
    per = cols // 128
    slots = cache_ref.shape[0]
    step = slots // chunks
    me = me_ref[0]
    copies, backs = [], []
    for c in range(chunks):
        part = pl.ds(c * step, step)
        copies.append(pltpu.make_async_copy(cache_ref.at[part], tiles.at[part], in_sems.at[c]))
        backs.append(pltpu.make_async_copy(fresh.at[part], out_ref.at[part], out_sems.at[c]))
        copies[-1].start()
    first = 3 * devices // 4
    last_row = 3 * heads * sessions
    flat[last_row : last_row + 8, :] = jnp.zeros((8, 128), F32)
    for j in range(devices):
        device = me ^ order[j]

        @pl.when(device < first)
        def _():
            base = pl.multiple_of(device * (per * sessions), 8)
            for b in range(per):
                flat[pl.ds(base + b * sessions, sessions), :] = pieces[j][
                    :, b * 128 : (b + 1) * 128
                ].astype(F32)

        @pl.when(device >= first)
        def _():
            gate_ref[device - first] = pieces[j][...]

    comp = heads * sessions

    @pl.loop(0, slots // 8)
    def _(group):
        for u in range(8):
            e = group * 8 + u
            row = slot_ref[0, e]
            query[pl.ds(e, 1), :] = flat[pl.ds(row, 1), :]
            keys[pl.ds(e, 1), :] = flat[pl.ds(jnp.minimum(row + comp, last_row), 1), :]
            values[pl.ds(e, 1), :] = flat[pl.ds(jnp.minimum(row + 2 * comp, last_row), 1), :]

    rows8 = lax.broadcasted_iota(I32, (8, 128), 0)

    def advance(group):
        base = pl.multiple_of(group * 8, 8)
        q8 = query[pl.ds(base, 8), :]
        k8 = keys[pl.ds(base, 8), :]
        v8 = values[pl.ds(base, 8), :]
        rate = jnp.zeros((8, 128), F32)
        scale = jnp.ones((8, 128), F32)
        for u in range(8):
            head = slot_ref[1, base + u]
            one = jnp.where(head < 0, 0.0, rate_ref[jnp.maximum(head, 0)])
            rate = jnp.where(rows8 == u, one, rate)
            scale = jnp.where(rows8 == u, scale_ref[base + u], scale)
        decay = jnp.exp(-rate)
        scaled = v8 * (1.0 / scale)
        high = scaled.astype(BF16)
        rest = scaled - high.astype(F32)
        middle = rest.astype(BF16)
        low = (rest - middle.astype(F32)).astype(BF16)
        zero = jnp.zeros((8, 128), BF16)
        spread = [
            jnp.concatenate([jnp.where(rows8 == u, t.astype(F32), 0.0) for u in range(8)], axis=1)
            for t in (high, middle, low, zero)
        ]
        spread = jnp.concatenate(spread, axis=0).astype(BF16)
        k32 = jnp.concatenate([k8, k8, k8, k8], axis=0).T.astype(BF16)
        outer = jnp.dot(k32, spread, preferred_element_type=F32)
        wide = jnp.concatenate([tiles[base + u] for u in range(8)], axis=1)
        prod = jnp.dot(q8.astype(BF16), wide, preferred_element_type=F32)
        seen = jnp.zeros((8, 128), F32)
        for u in range(8):
            part = slice(u * 128, (u + 1) * 128)
            seen = jnp.where(rows8 == u, prod[:, part], seen)
            fresh[base + u] = (
                decay[u : u + 1, :] * wide[:, part].astype(F32) + outer[:, part]
            ).astype(BF16)
        near = jnp.sum(q8 * k8, axis=1, keepdims=True)
        result = seen * (decay * scale) + near * v8
        for u in range(8):
            reads[pl.ds(slot_ref[2, base + u], 1), :] = result[u : u + 1, :]

    for c in range(chunks):
        copies[c].wait()
        pl.loop(c * (step // 8), (c + 1) * (step // 8))(advance)
        backs[c].start()
    entries = read_ref.shape[0]
    read_ref[...] = reads[:entries, :].astype(BF16)
    for back in backs:
        back.wait()


def advance_tiles(pieces, cache, me, slot, rate, scale, heads, capacity):
    devices = len(pieces)
    entries = devices * capacity
    sessions, cols = pieces[0].shape
    slots = cache.shape[0]
    chunks = 7 if slots % 56 == 0 else 1
    return pl.pallas_call(
        functools.partial(advance_kernel, devices, heads, chunks),
        out_shape=(
            jax.ShapeDtypeStruct((entries, 128), BF16),
            jax.ShapeDtypeStruct((devices // 4, sessions, cols), BF16),
            jax.ShapeDtypeStruct(cache.shape, BF16),
        ),
        in_specs=[SMEM] * 4 + [ANY] + [VMEM] * devices,
        out_specs=(VMEM, VMEM, ANY),
        scratch_shapes=[
            pltpu.VMEM((3 * heads * sessions + 8, 128), F32),
            pltpu.VMEM(cache.shape, BF16),
            pltpu.VMEM(cache.shape, BF16),
            pltpu.VMEM((slots, 128), F32),
            pltpu.VMEM((slots, 128), F32),
            pltpu.VMEM((slots, 128), F32),
            pltpu.VMEM((entries + 8, 128), F32),
            pltpu.SemaphoreType.DMA((chunks,)),
            pltpu.SemaphoreType.DMA((chunks,)),
        ],
        compiler_params=pltpu.CompilerParams(vmem_limit_bytes=VMEM_LIMIT),
        cost_estimate=pl.CostEstimate(
            flops=4 * cache.size, bytes_accessed=4 * cache.size, transcendentals=0
        ),
        name="advance",
    )(me, slot, rate, scale, cache, *pieces)


def finish_kernel(devices, *refs):
    me_ref, pick_ref, gate_ref, gain_ref, w_ref = refs[:5]
    pieces = refs[5 : 5 + devices]
    out_ref, flat, hidden, merged, wbuf, sem = refs[5 + devices :]
    order = block_order(devices)
    entries = pieces[0].shape[0]
    sessions = gate_ref.shape[1]
    per = gate_ref.shape[2] // 128
    heads = merged.shape[1] // 128
    me = me_ref[0]
    copy = pltpu.make_async_copy(w_ref, wbuf, sem)
    copy.start()
    for j in range(devices):
        base = pl.multiple_of((me ^ order[j]) * entries, 8)
        flat[pl.ds(base, entries), :] = pieces[j][...].astype(F32)

    @pl.loop(0, heads)
    def _(h):
        base = pl.multiple_of(h * sessions, 8)
        for s in range(sessions):
            hidden[pl.ds(base + s, 1), :] = flat[pl.ds(pick_ref[h, s], 1), :]

    squares = jnp.zeros((sessions, 128), F32)
    for h in range(heads):
        block = hidden[h * sessions : (h + 1) * sessions, :]
        squares += block * block
    mean = jnp.sum(squares, axis=1, keepdims=True) * (1.0 / (heads * 128))
    norm = lax.rsqrt(mean + 1e-6)
    for h in range(heads):
        block = hidden[h * sessions : (h + 1) * sessions, :]
        gate = gate_ref[h // per, :, (h % per) * 128 : (h % per + 1) * 128]
        block = block * norm * gain_ref[h : h + 1, :] * gate.astype(F32)
        merged[:, h * 128 : (h + 1) * 128] = block.astype(BF16)
    copy.wait()
    out_ref[...] = jnp.dot(merged[...], wbuf[...], preferred_element_type=F32).astype(BF16)


def finish(pieces, gates, me, pick, gain, w_out):
    devices = len(pieces)
    entries = pieces[0].shape[0]
    sessions = gates.shape[1]
    width = w_out.shape[0]
    return pl.pallas_call(
        functools.partial(finish_kernel, devices),
        out_shape=jax.ShapeDtypeStruct((sessions, w_out.shape[1]), BF16),
        in_specs=[SMEM, SMEM, VMEM, VMEM, ANY] + [VMEM] * devices,
        out_specs=VMEM,
        scratch_shapes=[
            pltpu.VMEM((devices * entries, 128), F32),
            pltpu.VMEM((sessions * width // 128, 128), F32),
            pltpu.VMEM((sessions, width), BF16),
            pltpu.VMEM(w_out.shape, BF16),
            pltpu.SemaphoreType.DMA,
        ],
        compiler_params=pltpu.CompilerParams(vmem_limit_bytes=VMEM_LIMIT),
        cost_estimate=pl.CostEstimate(
            flops=2 * sessions * w_out.size, bytes_accessed=2 * w_out.size, transcendentals=0
        ),
        name="finish",
    )(me, pick, gates, gain, w_out, *pieces)


def on_device(
    tokens,
    w_proj,
    w_out,
    decay_rate,
    norm_gain,
    cache_tiles,
    tile_scales,
    tile_holder,
    tile_rank,
    send_slot,
):
    devices = lax.axis_size("batch")
    me = lax.axis_index("batch").astype(I32).reshape(1)
    heads = decay_rate.shape[0]
    capacity = send_slot.shape[-1]
    slots = cache_tiles.shape[0]

    tokens_all = gather_pieces(pack(tokens, tile_holder, tile_rank), devices)
    act, pick, slot = project(tokens_all, w_proj, me, send_slot[0], heads, slots)
    act_all = gather_pieces(act, devices)
    read, gates, new_cache = advance_tiles(
        act_all, cache_tiles, me, slot, decay_rate, tile_scales, heads, capacity
    )
    read_all = gather_pieces(read, devices)
    mixed_out = finish(read_all, gates, me, pick, norm_gain.reshape(heads, 128), w_out)
    return (mixed_out, new_cache)


def solution(mesh):
    return jax.shard_map(
        on_device,
        mesh=mesh,
        in_specs=(
            P(("groups", "batch"), None),
            P(None, "batch"),
            P(None, "batch"),
            P(),
            P(),
            P(("groups", "batch"), None, None),
            P(("groups", "batch")),
            P(("groups", "batch"), None),
            P(("groups", "batch"), None),
            P(("groups", "batch"), None, None),
        ),
        out_specs=(P("groups", "batch"), P(("groups", "batch"), None, None)),
        check_vma=False,
    )
```

```python
import functools
import math

import jax
import jax.numpy as jnp
from jax import lax
from jax.experimental import pallas as pl
from jax.experimental.pallas import tpu as pltpu
from jax.sharding import PartitionSpec as P

BF16 = jnp.bfloat16
F32 = jnp.float32
I32 = jnp.int32
SMEM = pl.BlockSpec(memory_space=pltpu.SMEM)
VMEM = pl.BlockSpec(memory_space=pltpu.VMEM)
ANY = pl.BlockSpec(memory_space=pl.ANY)


def grant(*arrays):
    held = sum(math.prod(a.shape) * jnp.dtype(a.dtype).itemsize for a in arrays)
    most = 60 * 1024 * 1024
    return held + 6 * 1024 * 1024 if held < most // 2 else most


def block_order(devices):
    order, bit = [0], devices // 2
    while bit >= 1:
        order = order + [o ^ bit for o in order]
        bit //= 2
    return order


def place_of(crossed, devices):
    bits = devices.bit_length() - 1
    return sum(((crossed >> k) & 1) << (bits - 1 - k) for k in range(bits))


def gather_pieces(block, devices):
    held, bit = [block], devices // 2
    while bit >= 1:
        pairs = [(i, i ^ bit) for i in range(devices)]
        held = held + [lax.ppermute(piece, "batch", pairs) for piece in held]
        bit //= 2
    return held


def is_large(*arrays):
    return sum(math.prod(a.shape) * jnp.dtype(a.dtype).itemsize for a in arrays) > 6 * 1024 * 1024


def fetch(ref, stage):
    if not stage:
        return ref[...]
    copy = pltpu.make_async_copy(ref, *stage)
    copy.start()
    copy.wait()
    return stage[0][...]


def pack_kernel(heads, tokens_ref, holder_ref, rank_ref, out_ref):
    own, width = tokens_ref.shape
    parts = []
    for i in range(own):
        parts.append(holder_ref[i : i + 1, :].astype(F32))
        parts.append(rank_ref[i : i + 1, :].astype(F32))
        parts.append(jnp.zeros((1, 128 - 2 * heads), F32))
    parts.append(jnp.zeros((1, width - own * 128), F32))
    table = jnp.concatenate(parts, axis=1)
    block = jnp.concatenate([tokens_ref[...].astype(F32), table], axis=0)
    out_ref[...] = block.astype(BF16)


def pack(tokens, holder, rank):
    own, width = tokens.shape
    return pl.pallas_call(
        functools.partial(pack_kernel, holder.shape[1]),
        out_shape=jax.ShapeDtypeStruct((own + 1, width), BF16),
        in_specs=[VMEM] * 3,
        out_specs=VMEM,
        compiler_params=pltpu.CompilerParams(vmem_limit_bytes=grant(tokens)),
        cost_estimate=pl.CostEstimate(flops=20000000000, bytes_accessed=60000000, transcendentals=0),
        name="pack",
    )(tokens, holder, rank)


def project_kernel(devices, heads, slots, steps, *refs):
    send_ref, w_ref = refs[:2]
    pieces = refs[2 : 2 + devices]
    act_ref, pick_ref, slot_ref, rows = refs[2 + devices :]
    order = block_order(devices)
    sessions, cols = act_ref.shape
    per = cols // 128
    own = sessions // devices
    capacity = send_ref.shape[0]
    width = w_ref.shape[0]
    chunk = width // steps
    me = lax.axis_index("batch")
    lane = lax.broadcasted_iota(I32, (1, sessions), 1)
    target = jnp.zeros((1, sessions), I32)
    source = jnp.zeros((1, sessions), I32)
    indices = []
    for j in range(devices):
        block = pieces[j][...].astype(F32)
        rows[j * own : (j + 1) * own, :] = block[:own]
        for i in range(own):
            indices.append(block[own : own + 1, i * 128 : (i + 1) * 128])
        inside = (lane >= j * own) & (lane < (j + 1) * own)
        target = jnp.where(inside, lane + ((me ^ order[j]) - j) * own, target)
        source = jnp.where(inside, lane + (place_of(me ^ j, devices) - j) * own, source)
    grid_row = lax.broadcasted_iota(I32, (sessions, sessions), 0)
    place = (grid_row == target).astype(F32).astype(BF16)
    place_t = (grid_row == source).astype(F32).astype(BF16)

    table = jnp.concatenate(indices, axis=0)
    table = jnp.dot(table.T.astype(BF16), place_t, preferred_element_type=F32).astype(I32)
    holder = table[:heads]
    rank = table[heads : 2 * heads]
    owner = (lane * (65536 // own + 1)) >> 16
    pick_ref[...] = (place_of(holder ^ me, devices) * devices + owner) * capacity + rank

    owner_row = lax.broadcasted_iota(I32, (devices, sessions), 0)
    spread = (owner_row == owner).astype(F32).astype(BF16)
    sent = jnp.concatenate([send_ref[r].astype(F32) for r in range(capacity)], axis=0).astype(BF16)
    sent = jnp.dot(sent, spread, preferred_element_type=F32).astype(I32)
    slot = jnp.full((heads, sessions), -1, I32)
    for r in range(capacity):
        slot = jnp.where(rank == r, sent[r : r + 1, :], slot)
    slot = jnp.where(holder == me, slot, -1)
    entry = owner * capacity + rank
    padded = slot_ref.shape[1]
    slot_lane = lax.broadcasted_iota(I32, (heads, padded), 1)
    head_row = lax.broadcasted_iota(I32, (heads, padded), 0)
    piece = jnp.zeros((heads, padded), I32)
    for group in range(heads // per):
        inside = (head_row >= group * per) & (head_row < (group + 1) * per)
        piece = jnp.where(inside, place_of(me ^ group, devices), piece)
    found = jnp.zeros((heads, padded), I32)
    found_entry = jnp.zeros((heads, padded), I32)
    for s in range(sessions):
        same = slot[:, s : s + 1] == slot_lane
        found = jnp.where(same, s + 1, found)
        found_entry = jnp.where(same, entry[:, s : s + 1], found_entry)
    used = found > 0

    def only(x):
        return jnp.sum(jnp.where(used, x, 0).astype(F32), axis=0, keepdims=True).astype(I32)

    any_used = only(found) > 0
    head = only(head_row)
    piece = only(piece)
    inner = (head - only(head_row // per * per)) * sessions + only(found) - 1
    size = per * sessions
    unused = devices * size
    slot_ref[0:1, :] = jnp.where(any_used, piece * size + inner, unused)
    slot_ref[1:2, :] = jnp.where(any_used, (piece ^ 2) * size + inner, unused)
    slot_ref[2:3, :] = jnp.where(any_used, (piece ^ 1) * size + inner, unused)
    slot_ref[3:4, :] = jnp.where(any_used, head, -1)
    slot_ref[4:5, :] = jnp.where(any_used, only(found_entry), devices * capacity)
    slot_ref[5:8, :] = jnp.zeros((3, padded), I32)

    total = jnp.zeros(act_ref.shape, F32)
    for step in range(steps):
        part = slice(step * chunk, (step + 1) * chunk)
        total += jnp.dot(rows[:, part].astype(BF16), w_ref[part, :], preferred_element_type=F32)
    gate = jax.nn.sigmoid(total)
    is_gate = me * cols >= 3 * heads * 128
    active = jnp.where(is_gate, gate, total * gate).astype(BF16)
    act_ref[...] = jnp.dot(place, active, preferred_element_type=F32).astype(BF16)


def project(pieces, w, send, heads, slots):
    devices = len(pieces)
    own = pieces[0].shape[0] - 1
    sessions = own * devices
    width, cols = w.shape
    steps = 8
    padded = (slots + 127) // 128 * 128
    return pl.pallas_call(
        functools.partial(project_kernel, devices, heads, slots, steps),
        out_shape=(
            jax.ShapeDtypeStruct((sessions, cols), BF16),
            jax.ShapeDtypeStruct((heads, sessions), I32),
            jax.ShapeDtypeStruct((8, padded), I32),
        ),
        in_specs=[VMEM] * (2 + devices),
        out_specs=(VMEM, VMEM, VMEM),
        scratch_shapes=[
            pltpu.VMEM((sessions, width), F32),
        ],
        compiler_params=pltpu.CompilerParams(
            vmem_limit_bytes=grant(w, *pieces, jax.ShapeDtypeStruct((sessions, width), F32))
        ),
        cost_estimate=pl.CostEstimate(
            flops=2 * sessions * width * cols, bytes_accessed=2 * width * cols, transcendentals=0
        ),
        name="project",
    )(send, w, *pieces)


def advance_kernel(devices, chunks, *refs):
    slot_ref, rate_ref, scale_ref, cache_ref = refs[:4]
    pieces = refs[4 : 4 + devices]
    read_ref, flat_ref, out_ref, fresh, query, keys, values, reads, sems, *stage = refs[
        4 + devices :
    ]
    sessions, cols = pieces[0].shape
    per = cols // 128
    slots = cache_ref.shape[0]
    step = slots // chunks
    for j in range(devices):
        block = fetch(pieces[j], stage)
        for b in range(per):
            base = (j * per + b) * sessions
            flat_ref[base : base + sessions, :] = block[:, b * 128 : (b + 1) * 128].astype(F32)
    base = devices * per * sessions
    flat_ref[base : base + 8, :] = jnp.zeros((8, 128), F32)

    @pl.loop(0, slots // 8)
    def _(group):
        for u in range(8):
            e = group * 8 + u
            query[pl.ds(e, 1), :] = flat_ref[pl.ds(slot_ref[0, e], 1), :]
            keys[pl.ds(e, 1), :] = flat_ref[pl.ds(slot_ref[1, e], 1), :]
            values[pl.ds(e, 1), :] = flat_ref[pl.ds(slot_ref[2, e], 1), :]

    rows8 = lax.broadcasted_iota(I32, (8, 128), 0)

    def advance(base):
        q8 = query[base : base + 8, :]
        k8 = keys[base : base + 8, :]
        v8 = values[base : base + 8, :]
        rate = jnp.zeros((8, 128), F32)
        scale = jnp.ones((8, 128), F32)
        for u in range(8):
            head = slot_ref[3, base + u]
            one = jnp.where(head < 0, 0.0, rate_ref[jnp.maximum(head, 0)])
            rate = jnp.where(rows8 == u, one, rate)
            scale = jnp.where(rows8 == u, scale_ref[base + u], scale)
        decay = jnp.exp(-rate)
        scaled = v8 * (1.0 / scale)
        columns = k8.T
        wide = jnp.concatenate([cache_ref[base + u] for u in range(8)], axis=1)
        prod = jnp.dot(q8.astype(BF16), wide, preferred_element_type=F32)
        seen = jnp.zeros((8, 128), F32)
        for u in range(8):
            seen = jnp.where(rows8 == u, prod[:, u * 128 : (u + 1) * 128], seen)
            fresh[base + u] = (
                decay[u : u + 1, :] * cache_ref[base + u].astype(F32)
                + columns[:, u : u + 1] * scaled[u : u + 1, :]
            ).astype(BF16)
        near = jnp.sum(q8 * k8, axis=1, keepdims=True)
        result = seen * (decay * scale) + near * v8
        for u in range(8):
            reads[pl.ds(slot_ref[4, base + u], 1), :] = result[u : u + 1, :]

    backs = []
    for c in range(chunks):
        for base in range(c * step, (c + 1) * step, 8):
            advance(base)
        part = pl.ds(c * step, step)
        backs.append(pltpu.make_async_copy(fresh.at[part], out_ref.at[part], sems.at[c]))
        backs[-1].start()
    entries = read_ref.shape[0]
    read_ref[...] = reads[:entries, :].astype(BF16)
    for back in backs:
        back.wait()


def advance_tiles(pieces, cache, slot, rate, scale, capacity):
    devices = len(pieces)
    entries = devices * capacity
    sessions, cols = pieces[0].shape
    slots = cache.shape[0]
    chunks = 7 if slots % 56 == 0 else 1
    large = is_large(*pieces)
    flat = jax.ShapeDtypeStruct((devices * sessions * cols // 128 + 8, 128), F32)
    return pl.pallas_call(
        functools.partial(advance_kernel, devices, chunks),
        out_shape=(
            jax.ShapeDtypeStruct((entries, 128), BF16),
            flat,
            jax.ShapeDtypeStruct(cache.shape, BF16),
        ),
        in_specs=[SMEM] * 3 + [VMEM] + [ANY if large else VMEM] * devices,
        out_specs=(VMEM, VMEM, ANY),
        scratch_shapes=[
            pltpu.VMEM(cache.shape, BF16),
            pltpu.VMEM((slots, 128), F32),
            pltpu.VMEM((slots, 128), F32),
            pltpu.VMEM((slots, 128), F32),
            pltpu.VMEM((entries + 8, 128), F32),
            pltpu.SemaphoreType.DMA((chunks,)),
        ]
        + ([pltpu.VMEM((sessions, cols), BF16), pltpu.SemaphoreType.DMA] if large else []),
        compiler_params=pltpu.CompilerParams(
            vmem_limit_bytes=grant(cache, cache, flat, *([] if large else pieces))
        ),
        cost_estimate=pl.CostEstimate(
            flops=4 * cache.size, bytes_accessed=4 * cache.size, transcendentals=0
        ),
        name="advance",
    )(slot, rate, scale, cache, *pieces)


def finish_kernel(devices, per, *refs):
    pick_ref, act_ref, gain_ref, w_ref = refs[:4]
    pieces = refs[4 : 4 + devices]
    out_ref, flat, hidden, merged, *stages = refs[4 + devices :]
    entries = pieces[0].shape[0]
    sessions = merged.shape[0]
    heads = merged.shape[1] // 128
    me = lax.axis_index("batch")
    for j in range(devices):
        flat[j * entries : (j + 1) * entries, :] = fetch(pieces[j], stages[:2]).astype(F32)

    @pl.loop(0, heads)
    def _(h):
        base = pl.multiple_of(h * sessions, 8)
        for s in range(sessions):
            hidden[pl.ds(base + s, 1), :] = flat[pl.ds(pick_ref[h, s], 1), :]

    squares = jnp.zeros((sessions, 128), F32)
    for h in range(heads):
        block = hidden[h * sessions : (h + 1) * sessions, :]
        squares += block * block
    mean = jnp.sum(squares, axis=1, keepdims=True) * (1.0 / (heads * 128))
    norm = lax.rsqrt(mean + 1e-6)
    for h in range(heads):
        block = hidden[h * sessions : (h + 1) * sessions, :]
        piece = place_of(me ^ (3 * devices // 4 + h // per), devices)
        base = pl.multiple_of((piece * per + h % per) * sessions, 8)
        gate = fetch(act_ref.at[pl.ds(base, sessions)], stages[2:])
        block = block * norm * gain_ref[h : h + 1, :] * gate
        merged[:, h * 128 : (h + 1) * 128] = block.astype(BF16)
    out_ref[...] = jnp.dot(merged[...], w_ref[...], preferred_element_type=F32).astype(BF16)


def finish(pieces, gates, pick, gain, w_out):
    devices = len(pieces)
    entries = pieces[0].shape[0]
    heads, sessions = pick.shape
    per = gates.shape[0] // (devices * sessions)
    large = is_large(gates)
    width = w_out.shape[0]
    return pl.pallas_call(
        functools.partial(finish_kernel, devices, per),
        out_shape=jax.ShapeDtypeStruct((sessions, w_out.shape[1]), BF16),
        in_specs=[SMEM, ANY if large else VMEM, VMEM, VMEM] + [ANY if large else VMEM] * devices,
        out_specs=VMEM,
        scratch_shapes=[
            pltpu.VMEM((devices * entries, 128), F32),
            pltpu.VMEM((sessions * width // 128, 128), F32),
            pltpu.VMEM((sessions, width), BF16),
        ]
        + (
            [
                pltpu.VMEM((entries, 128), BF16),
                pltpu.SemaphoreType.DMA,
                pltpu.VMEM((sessions, 128), F32),
                pltpu.SemaphoreType.DMA,
            ]
            if large
            else []
        ),
        compiler_params=pltpu.CompilerParams(
            vmem_limit_bytes=grant(
                w_out,
                *([] if large else [gates, *pieces]),
                jax.ShapeDtypeStruct((devices * entries, 128), F32),
                jax.ShapeDtypeStruct((sessions * width // 128, 192), F32),
            )
        ),
        cost_estimate=pl.CostEstimate(
            flops=2 * sessions * w_out.size, bytes_accessed=2 * w_out.size, transcendentals=0
        ),
        name="finish",
    )(pick, gates, gain, w_out, *pieces)


def on_device(
    tokens,
    w_proj,
    w_out,
    decay_rate,
    norm_gain,
    cache_tiles,
    tile_scales,
    tile_holder,
    tile_rank,
    send_slot,
):
    devices = lax.axis_size("batch")
    heads = decay_rate.shape[0]
    capacity = send_slot.shape[-1]
    slots = cache_tiles.shape[0]

    tokens_all = gather_pieces(pack(tokens, tile_holder, tile_rank), devices)
    act, pick, slot = project(
        tokens_all, w_proj, jnp.transpose(send_slot, (2, 0, 1)), heads, slots
    )
    act_all = gather_pieces(act, devices)
    read, gates, new_cache = advance_tiles(
        act_all, cache_tiles, slot, decay_rate, tile_scales, capacity
    )
    read_all = gather_pieces(read, devices)
    mixed_out = finish(read_all, gates, pick, norm_gain.reshape(heads, 128), w_out)
    return (mixed_out, new_cache)


def solution(mesh):
    return jax.shard_map(
        on_device,
        mesh=mesh,
        in_specs=(
            P(("groups", "batch"), None),
            P(None, "batch"),
            P(None, "batch"),
            P(),
            P(),
            P(("groups", "batch"), None, None),
            P(("groups", "batch")),
            P(("groups", "batch"), None),
            P(("groups", "batch"), None),
            P(("groups", "batch"), None, None),
        ),
        out_specs=(P("groups", "batch"), P(("groups", "batch"), None, None)),
        check_vma=False,
    )
```

```python
import functools
import math

import jax
import jax.numpy as jnp
from jax import lax
from jax.experimental import pallas as pl
from jax.experimental.pallas import tpu as pltpu
from jax.sharding import PartitionSpec as P

BF16 = jnp.bfloat16
F32 = jnp.float32
I32 = jnp.int32
SMEM = pl.BlockSpec(memory_space=pltpu.SMEM)
VMEM = pl.BlockSpec(memory_space=pltpu.VMEM)
ANY = pl.BlockSpec(memory_space=pl.ANY)


def grant(*arrays):
    held = sum(math.prod(a.shape) * jnp.dtype(a.dtype).itemsize for a in arrays)
    most = 60 * 1024 * 1024
    return held + 6 * 1024 * 1024 if held < most // 2 else most


def block_order(devices):
    order, bit = [0], devices // 2
    while bit >= 1:
        order = order + [o ^ bit for o in order]
        bit //= 2
    return order


def place_of(crossed, devices):
    bits = devices.bit_length() - 1
    return sum(((crossed >> k) & 1) << (bits - 1 - k) for k in range(bits))


def cross(piece, bit, devices):
    return lax.ppermute(piece, "batch", [(i, i ^ bit) for i in range(devices)])


def gather_pieces(block, devices):
    held, bit = [block], devices // 2
    while bit >= 1:
        held = held + [cross(piece, bit, devices) for piece in held]
        bit //= 2
    return held


def is_large(*arrays):
    return sum(math.prod(a.shape) * jnp.dtype(a.dtype).itemsize for a in arrays) > 6 * 1024 * 1024


def fetch(ref, stage):
    if not stage:
        return ref[...]
    copy = pltpu.make_async_copy(ref, *stage)
    copy.start()
    copy.wait()
    return stage[0][...]


def pack_kernel(heads, tokens_ref, holder_ref, rank_ref, out_ref):
    own, width = tokens_ref.shape
    parts = []
    for i in range(own):
        parts.append(holder_ref[i : i + 1, :].astype(F32))
        parts.append(rank_ref[i : i + 1, :].astype(F32))
        parts.append(jnp.zeros((1, 128 - 2 * heads), F32))
    parts.append(jnp.zeros((1, width - own * 128), F32))
    table = jnp.concatenate(parts, axis=1)
    block = jnp.concatenate([tokens_ref[...].astype(F32), table], axis=0)
    out_ref[...] = block.astype(BF16)


def pack(tokens, holder, rank):
    own, width = tokens.shape
    return pl.pallas_call(
        functools.partial(pack_kernel, holder.shape[1]),
        out_shape=jax.ShapeDtypeStruct((own + 1, width), BF16),
        in_specs=[VMEM] * 3,
        out_specs=VMEM,
        compiler_params=pltpu.CompilerParams(vmem_limit_bytes=grant(tokens)),
        cost_estimate=pl.CostEstimate(flops=20000000000, bytes_accessed=60000000, transcendentals=0),
        name="pack",
    )(tokens, holder, rank)


def project_kernel(devices, heads, slots, steps, *refs):
    send_ref, w_ref = refs[:2]
    pieces = refs[2 : 2 + devices]
    act_ref, pick_ref, slot_ref, rows = refs[2 + devices :]
    order = block_order(devices)
    sessions, cols = act_ref.shape
    per = cols // 128
    own = sessions // devices
    capacity = send_ref.shape[0]
    width = w_ref.shape[0]
    chunk = width // steps
    me = lax.axis_index("batch")
    lane = lax.broadcasted_iota(I32, (1, sessions), 1)
    target = jnp.zeros((1, sessions), I32)
    source = jnp.zeros((1, sessions), I32)
    indices = []
    for j in range(devices):
        block = pieces[j][...].astype(F32)
        rows[j * own : (j + 1) * own, :] = block[:own]
        for i in range(own):
            indices.append(block[own : own + 1, i * 128 : (i + 1) * 128])
        inside = (lane >= j * own) & (lane < (j + 1) * own)
        target = jnp.where(inside, lane + ((me ^ order[j]) - j) * own, target)
        source = jnp.where(inside, lane + (place_of(me ^ j, devices) - j) * own, source)
    grid_row = lax.broadcasted_iota(I32, (sessions, sessions), 0)
    place = (grid_row == target).astype(F32).astype(BF16)
    place_t = (grid_row == source).astype(F32).astype(BF16)

    table = jnp.concatenate(indices, axis=0)
    table = jnp.dot(table.T.astype(BF16), place_t, preferred_element_type=F32).astype(I32)
    holder = table[:heads]
    rank = table[heads : 2 * heads]
    owner = (lane * (65536 // own + 1)) >> 16
    pick_ref[...] = (place_of(holder ^ me, devices) * devices + owner) * capacity + rank

    owner_row = lax.broadcasted_iota(I32, (devices, sessions), 0)
    spread = (owner_row == owner).astype(F32).astype(BF16)
    sent = jnp.concatenate([send_ref[r].astype(F32) for r in range(capacity)], axis=0).astype(BF16)
    sent = jnp.dot(sent, spread, preferred_element_type=F32).astype(I32)
    slot = jnp.full((heads, sessions), -1, I32)
    for r in range(capacity):
        slot = jnp.where(rank == r, sent[r : r + 1, :], slot)
    slot = jnp.where(holder == me, slot, -1)
    entry = owner * capacity + rank
    padded = slot_ref.shape[1]
    slot_lane = lax.broadcasted_iota(I32, (heads, padded), 1)
    head_row = lax.broadcasted_iota(I32, (heads, padded), 0)
    piece = jnp.zeros((heads, padded), I32)
    for group in range(heads // per):
        inside = (head_row >= group * per) & (head_row < (group + 1) * per)
        piece = jnp.where(inside, place_of(me ^ group, devices), piece)
    found = jnp.zeros((heads, padded), I32)
    found_entry = jnp.zeros((heads, padded), I32)
    for s in range(sessions):
        same = slot[:, s : s + 1] == slot_lane
        found = jnp.where(same, s + 1, found)
        found_entry = jnp.where(same, entry[:, s : s + 1], found_entry)
    used = found > 0

    def only(x):
        return jnp.sum(jnp.where(used, x, 0).astype(F32), axis=0, keepdims=True).astype(I32)

    any_used = only(found) > 0
    head = only(head_row)
    piece = only(piece)
    inner = (head - only(head_row // per * per)) * sessions + only(found) - 1
    size = per * sessions
    unused = devices * size
    slot_ref[0:1, :] = jnp.where(any_used, piece * size + inner, unused)
    slot_ref[1:2, :] = jnp.where(any_used, (piece ^ 2) * size + inner, unused)
    slot_ref[2:3, :] = jnp.where(any_used, (piece ^ 1) * size + inner, unused)
    slot_ref[3:4, :] = jnp.where(any_used, head, -1)
    slot_ref[4:5, :] = jnp.where(any_used, only(found_entry), devices * capacity)
    slot_ref[5:8, :] = jnp.zeros((3, padded), I32)

    total = jnp.zeros(act_ref.shape, F32)
    for step in range(steps):
        part = slice(step * chunk, (step + 1) * chunk)
        total += jnp.dot(rows[:, part].astype(BF16), w_ref[part, :], preferred_element_type=F32)
    gate = jax.nn.sigmoid(total)
    is_gate = me * cols >= 3 * heads * 128
    active = jnp.where(is_gate, gate, total * gate).astype(BF16)
    act_ref[...] = jnp.dot(place, active, preferred_element_type=F32).astype(BF16)


def project(pieces, w, send, heads, slots):
    devices = len(pieces)
    own = pieces[0].shape[0] - 1
    sessions = own * devices
    width, cols = w.shape
    steps = 8
    padded = (slots + 127) // 128 * 128
    return pl.pallas_call(
        functools.partial(project_kernel, devices, heads, slots, steps),
        out_shape=(
            jax.ShapeDtypeStruct((sessions, cols), BF16),
            jax.ShapeDtypeStruct((heads, sessions), I32),
            jax.ShapeDtypeStruct((8, padded), I32),
        ),
        in_specs=[VMEM] * (2 + devices),
        out_specs=(VMEM, VMEM, VMEM),
        scratch_shapes=[
            pltpu.VMEM((sessions, width), F32),
        ],
        compiler_params=pltpu.CompilerParams(
            vmem_limit_bytes=grant(w, *pieces, jax.ShapeDtypeStruct((sessions, width), F32))
        ),
        cost_estimate=pl.CostEstimate(
            flops=2 * sessions * width * cols, bytes_accessed=2 * width * cols, transcendentals=0
        ),
        name="project",
    )(send, w, *pieces)


def readout_kernel(devices, *refs):
    slot_ref, rate_ref, scale_ref, cache_ref = refs[:4]
    pieces = refs[4 : 4 + devices]
    read_ref, flat_ref, key_ref, value_ref, query, reads, *stage = refs[4 + devices :]
    sessions, cols = pieces[0].shape
    per = cols // 128
    slots = cache_ref.shape[0]
    for j in range(devices):
        block = fetch(pieces[j], stage)
        for b in range(per):
            base = (j * per + b) * sessions
            flat_ref[base : base + sessions, :] = block[:, b * 128 : (b + 1) * 128].astype(F32)
    base = devices * per * sessions
    flat_ref[base : base + 8, :] = jnp.zeros((8, 128), F32)

    @pl.loop(0, slots // 8)
    def _(group):
        for u in range(8):
            e = group * 8 + u
            query[pl.ds(e, 1), :] = flat_ref[pl.ds(slot_ref[0, e], 1), :]
            key_ref[pl.ds(e, 1), :] = flat_ref[pl.ds(slot_ref[1, e], 1), :]
            value_ref[pl.ds(e, 1), :] = flat_ref[pl.ds(slot_ref[2, e], 1), :]

    rows8 = lax.broadcasted_iota(I32, (8, 128), 0)
    for base in range(0, slots, 8):
        q8 = query[base : base + 8, :]
        decay, scale = factors(slot_ref, rate_ref, scale_ref, base)
        wide = jnp.concatenate([cache_ref[base + u] for u in range(8)], axis=1)
        prod = jnp.dot(q8.astype(BF16), wide, preferred_element_type=F32)
        seen = jnp.zeros((8, 128), F32)
        for u in range(8):
            seen = jnp.where(rows8 == u, prod[:, u * 128 : (u + 1) * 128], seen)
        near = jnp.sum(q8 * key_ref[base : base + 8, :], axis=1, keepdims=True)
        result = seen * (decay * scale) + near * value_ref[base : base + 8, :]
        for u in range(8):
            reads[pl.ds(slot_ref[4, base + u], 1), :] = result[u : u + 1, :]
    entries = read_ref.shape[0]
    read_ref[...] = reads[:entries, :].astype(BF16)


def factors(slot_ref, rate_ref, scale_ref, base):
    rows8 = lax.broadcasted_iota(I32, (8, 128), 0)
    rate = jnp.zeros((8, 128), F32)
    scale = jnp.ones((8, 128), F32)
    for u in range(8):
        head = slot_ref[3, base + u]
        one = jnp.where(head < 0, 0.0, rate_ref[jnp.maximum(head, 0)])
        rate = jnp.where(rows8 == u, one, rate)
        scale = jnp.where(rows8 == u, scale_ref[base + u], scale)
    return jnp.exp(-rate), scale


def read_states(pieces, cache, slot, rate, scale, capacity):
    devices = len(pieces)
    entries = devices * capacity
    sessions, cols = pieces[0].shape
    slots = cache.shape[0]
    large = is_large(*pieces)
    flat = jax.ShapeDtypeStruct((devices * sessions * cols // 128 + 8, 128), F32)
    rows = jax.ShapeDtypeStruct((slots, 128), F32)
    return pl.pallas_call(
        functools.partial(readout_kernel, devices),
        out_shape=(jax.ShapeDtypeStruct((entries, 128), BF16), flat, rows, rows),
        in_specs=[SMEM] * 3 + [VMEM] + [ANY if large else VMEM] * devices,
        out_specs=(VMEM, VMEM, VMEM, VMEM),
        scratch_shapes=[
            pltpu.VMEM((slots, 128), F32),
            pltpu.VMEM((entries + 8, 128), F32),
        ]
        + ([pltpu.VMEM((sessions, cols), BF16), pltpu.SemaphoreType.DMA] if large else []),
        compiler_params=pltpu.CompilerParams(
            vmem_limit_bytes=grant(cache, flat, *([] if large else pieces))
        ),
        cost_estimate=pl.CostEstimate(
            flops=2 * cache.size, bytes_accessed=8 * cache.size, transcendentals=0
        ),
        name="readout",
    )(slot, rate, scale, cache, *pieces)


def update_kernel(first, count, *refs):
    slot_ref, rate_ref, scale_ref, cache_ref, key_ref, value_ref = refs[:6]
    out_ref, fresh, sems = refs[-3:]
    rows8 = lax.broadcasted_iota(I32, (8, 128), 0)
    backs = []
    for base in range(first, first + count, 8):
        decay, scale = factors(slot_ref, rate_ref, scale_ref, base)
        scaled = value_ref[base : base + 8, :] * (1.0 / scale)
        high = scaled.astype(BF16).astype(F32)
        spread = jnp.concatenate(
            [
                jnp.concatenate([jnp.where(rows8 == u, term, 0.0) for u in range(8)], axis=1)
                for term in (high, scaled - high)
            ],
            axis=0,
        ).astype(BF16)
        columns = jnp.concatenate([key_ref[base : base + 8, :]] * 2, axis=0).T.astype(BF16)
        outer = jnp.dot(columns, spread, preferred_element_type=F32)
        for u in range(8):
            fresh[base - first + u] = (
                decay[u : u + 1, :] * cache_ref[base + u].astype(F32)
                + outer[:, u * 128 : (u + 1) * 128]
            ).astype(BF16)
        backs.append(
            pltpu.make_async_copy(
                fresh.at[pl.ds(base - first, 8)],
                out_ref.at[pl.ds(base, 8)],
                sems.at[(base - first) // 8],
            )
        )
        backs[-1].start()
    for back in backs:
        back.wait()


def update_tiles(cache, key_rows, values, slot, rate, scale, first, count, begun):
    return pl.pallas_call(
        functools.partial(update_kernel, first, count),
        out_shape=jax.ShapeDtypeStruct(cache.shape, BF16),
        in_specs=[SMEM] * 3 + [VMEM] * 3 + [ANY] * len(begun),
        out_specs=ANY,
        scratch_shapes=[
            pltpu.VMEM((count, 128, 128), BF16),
            pltpu.SemaphoreType.DMA((count // 8,)),
        ],
        input_output_aliases={6: 0} if begun else {},
        compiler_params=pltpu.CompilerParams(vmem_limit_bytes=grant(cache, cache)),
        cost_estimate=pl.CostEstimate(
            flops=0, bytes_accessed=4 * count * 128 * 128, transcendentals=0
        ),
        name="update",
    )(slot, rate, scale, cache, key_rows, values, *begun)


def finish_kernel(devices, per, *refs):
    pick_ref, act_ref, gain_ref, w_ref = refs[:4]
    pieces = refs[4 : 4 + devices]
    out_ref, flat, hidden, merged, *stages = refs[4 + devices :]
    entries = pieces[0].shape[0]
    sessions = merged.shape[0]
    heads = merged.shape[1] // 128
    me = lax.axis_index("batch")
    for j in range(devices):
        flat[j * entries : (j + 1) * entries, :] = fetch(pieces[j], stages[:2]).astype(F32)

    @pl.loop(0, heads)
    def _(h):
        base = pl.multiple_of(h * sessions, 8)
        for s in range(sessions):
            hidden[pl.ds(base + s, 1), :] = flat[pl.ds(pick_ref[h, s], 1), :]

    squares = jnp.zeros((sessions, 128), F32)
    for h in range(heads):
        block = hidden[h * sessions : (h + 1) * sessions, :]
        squares += block * block
    mean = jnp.sum(squares, axis=1, keepdims=True) * (1.0 / (heads * 128))
    norm = lax.rsqrt(mean + 1e-6)
    for h in range(heads):
        block = hidden[h * sessions : (h + 1) * sessions, :]
        piece = place_of(me ^ (3 * devices // 4 + h // per), devices)
        base = pl.multiple_of((piece * per + h % per) * sessions, 8)
        gate = fetch(act_ref.at[pl.ds(base, sessions)], stages[2:])
        block = block * norm * gain_ref[h : h + 1, :] * gate
        merged[:, h * 128 : (h + 1) * 128] = block.astype(BF16)
    out_ref[...] = jnp.dot(merged[...], w_ref[...], preferred_element_type=F32).astype(BF16)


def finish(pieces, gates, pick, gain, w_out):
    devices = len(pieces)
    entries = pieces[0].shape[0]
    heads, sessions = pick.shape
    per = gates.shape[0] // (devices * sessions)
    large = is_large(gates)
    width = w_out.shape[0]
    return pl.pallas_call(
        functools.partial(finish_kernel, devices, per),
        out_shape=jax.ShapeDtypeStruct((sessions, w_out.shape[1]), BF16),
        in_specs=[SMEM, ANY if large else VMEM, VMEM, VMEM] + [ANY if large else VMEM] * devices,
        out_specs=VMEM,
        scratch_shapes=[
            pltpu.VMEM((devices * entries, 128), F32),
            pltpu.VMEM((sessions * width // 128, 128), F32),
            pltpu.VMEM((sessions, width), BF16),
        ]
        + (
            [
                pltpu.VMEM((entries, 128), BF16),
                pltpu.SemaphoreType.DMA,
                pltpu.VMEM((sessions, 128), F32),
                pltpu.SemaphoreType.DMA,
            ]
            if large
            else []
        ),
        compiler_params=pltpu.CompilerParams(
            vmem_limit_bytes=grant(
                w_out,
                *([] if large else [gates, *pieces]),
                jax.ShapeDtypeStruct((devices * entries, 128), F32),
                jax.ShapeDtypeStruct((sessions * width // 128, 192), F32),
            )
        ),
        cost_estimate=pl.CostEstimate(
            flops=2 * sessions * w_out.size, bytes_accessed=2 * w_out.size, transcendentals=0
        ),
        name="finish",
    )(pick, gates, gain, w_out, *pieces)


def on_device(
    tokens,
    w_proj,
    w_out,
    decay_rate,
    norm_gain,
    cache_tiles,
    tile_scales,
    tile_holder,
    tile_rank,
    send_slot,
):
    devices = lax.axis_size("batch")
    heads = decay_rate.shape[0]
    capacity = send_slot.shape[-1]
    slots = cache_tiles.shape[0]

    tokens_all = gather_pieces(pack(tokens, tile_holder, tile_rank), devices)
    act, pick, slot = project(
        tokens_all, w_proj, jnp.transpose(send_slot, (2, 0, 1)), heads, slots
    )
    act_all = gather_pieces(act, devices)
    read, gates, key_rows, values = read_states(
        act_all, cache_tiles, slot, decay_rate, tile_scales, capacity
    )
    half = slots // 16 * 8
    update = functools.partial(
        update_tiles, cache_tiles, key_rows, values, slot, decay_rate, tile_scales
    )
    bits = [1 << k for k in reversed(range(1, devices.bit_length() - 1))]
    first = [cross(read, bit, devices) for bit in bits]
    new_cache = update(0, half, [])
    *first, new_cache = lax.optimization_barrier((*first, new_cache))
    held = [read]
    for own_piece, bit in zip(first, bits):
        last = [cross(piece, bit, devices) for piece in held[1:]]
        held = held + [own_piece] + last
    new_cache = update(half, slots - half, [new_cache])
    *last, new_cache = lax.optimization_barrier((*last, new_cache))
    held = held[: len(held) - len(last)] + last
    read_all = held + [cross(piece, 1, devices) for piece in held]
    mixed_out = finish(read_all, gates, pick, norm_gain.reshape(heads, 128), w_out)
    return (mixed_out, new_cache)


def solution(mesh):
    return jax.shard_map(
        on_device,
        mesh=mesh,
        in_specs=(
            P(("groups", "batch"), None),
            P(None, "batch"),
            P(None, "batch"),
            P(),
            P(),
            P(("groups", "batch"), None, None),
            P(("groups", "batch")),
            P(("groups", "batch"), None),
            P(("groups", "batch"), None),
            P(("groups", "batch"), None, None),
        ),
        out_specs=(P("groups", "batch"), P(("groups", "batch"), None, None)),
        check_vma=False,
    )
```

```python
import functools
import math

import jax
import jax.numpy as jnp
from jax import lax
from jax.experimental import pallas as pl
from jax.experimental.pallas import tpu as pltpu
from jax.sharding import PartitionSpec as P

BF16 = jnp.bfloat16
F32 = jnp.float32
I32 = jnp.int32
SMEM = pl.BlockSpec(memory_space=pltpu.SMEM)
VMEM = pl.BlockSpec(memory_space=pltpu.VMEM)
ANY = pl.BlockSpec(memory_space=pl.ANY)


def grant(*arrays):
    held = sum(math.prod(a.shape) * jnp.dtype(a.dtype).itemsize for a in arrays)
    most = 60 * 1024 * 1024
    return held + 6 * 1024 * 1024 if held < most // 2 else most


def block_order(devices):
    order, bit = [0], devices // 2
    while bit >= 1:
        order = order + [o ^ bit for o in order]
        bit //= 2
    return order


def place_of(crossed, devices):
    bits = devices.bit_length() - 1
    return sum(((crossed >> k) & 1) << (bits - 1 - k) for k in range(bits))


def cross(piece, bit, devices):
    return lax.ppermute(piece, "batch", [(i, i ^ bit) for i in range(devices)])


def gather_pieces(held, bit, devices):
    while bit >= 1:
        held = held + [cross(piece, bit, devices) for piece in held]
        bit //= 2
    return held


def is_large(*arrays):
    return sum(math.prod(a.shape) * jnp.dtype(a.dtype).itemsize for a in arrays) > 6 * 1024 * 1024


def fetch(ref, stage):
    if not stage:
        return ref[...]
    copy = pltpu.make_async_copy(ref, *stage)
    copy.start()
    copy.wait()
    return stage[0][...]


def pack_kernel(tokens_ref, origin_ref, out_ref):
    own, width = tokens_ref.shape
    heads = origin_ref.shape[1]
    parts = []
    for i in range(own):
        parts.append(origin_ref[i : i + 1, :].astype(F32))
        parts.append(jnp.zeros((1, 128 - heads), F32))
    parts.append(jnp.zeros((1, width - own * 128), F32))
    table = jnp.concatenate(parts, axis=1)
    block = jnp.concatenate([tokens_ref[...].astype(F32), table], axis=0)
    out_ref[...] = block.astype(BF16)


def pack(tokens, origin):
    own, width = tokens.shape
    return pl.pallas_call(
        pack_kernel,
        out_shape=jax.ShapeDtypeStruct((own + 1, width), BF16),
        in_specs=[VMEM] * 2,
        out_specs=VMEM,
        compiler_params=pltpu.CompilerParams(vmem_limit_bytes=grant(tokens)),
        cost_estimate=pl.CostEstimate(flops=20000000000, bytes_accessed=60000000, transcendentals=0),
        name="pack",
    )(tokens, origin)


def project_kernel(devices, heads, slots, steps, *refs):
    send_ref, w_ref = refs[:2]
    pieces = refs[2 : 2 + devices]
    act_ref, pick_ref, slot_ref, rows = refs[2 + devices :]
    order = block_order(devices)
    sessions, cols = act_ref.shape
    per = cols // 128
    own = sessions // devices
    capacity = send_ref.shape[0]
    width = w_ref.shape[0]
    chunk = width // steps
    me = lax.axis_index("batch")
    lane = lax.broadcasted_iota(I32, (1, sessions), 1)
    target = jnp.zeros((1, sessions), I32)
    source = jnp.zeros((1, sessions), I32)
    indices = []
    for j in range(devices):
        block = pieces[j][...].astype(F32)
        rows[j * own : (j + 1) * own, :] = block[:own]
        for i in range(own):
            indices.append(block[own : own + 1, i * 128 : (i + 1) * 128])
        inside = (lane >= j * own) & (lane < (j + 1) * own)
        target = jnp.where(inside, lane + ((me ^ order[j]) - j) * own, target)
        source = jnp.where(inside, lane + (place_of(me ^ j, devices) - j) * own, source)
    grid_row = lax.broadcasted_iota(I32, (sessions, sessions), 0)
    place = (grid_row == target).astype(F32).astype(BF16)
    place_t = (grid_row == source).astype(F32).astype(BF16)

    table = jnp.concatenate(indices, axis=0)
    table = jnp.dot(table.T.astype(BF16), place_t, preferred_element_type=F32).astype(I32)
    origin = table[:heads]
    holder = (origin * (65536 // capacity + 1)) >> 16
    rank = origin - holder * capacity
    owner = (lane * (65536 // own + 1)) >> 16
    pick_ref[...] = (place_of(holder ^ me, devices) * devices + owner) * capacity + rank

    owner_row = lax.broadcasted_iota(I32, (devices, sessions), 0)
    spread = (owner_row == owner).astype(F32).astype(BF16)
    sent = jnp.concatenate([send_ref[r].astype(F32) for r in range(capacity)], axis=0).astype(BF16)
    sent = jnp.dot(sent, spread, preferred_element_type=F32).astype(I32)
    slot = jnp.full((heads, sessions), -1, I32)
    for r in range(capacity):
        slot = jnp.where(rank == r, sent[r : r + 1, :], slot)
    slot = jnp.where(holder == me, slot, -1)
    entry = owner * capacity + rank
    padded = slot_ref.shape[1]
    slot_lane = lax.broadcasted_iota(I32, (heads, padded), 1)
    head_row = lax.broadcasted_iota(I32, (heads, padded), 0)
    piece = jnp.zeros((heads, padded), I32)
    for group in range(heads // per):
        inside = (head_row >= group * per) & (head_row < (group + 1) * per)
        piece = jnp.where(inside, place_of(me ^ group, devices), piece)
    found = jnp.zeros((heads, padded), I32)
    found_entry = jnp.zeros((heads, padded), I32)
    for s in range(sessions):
        same = slot[:, s : s + 1] == slot_lane
        found = jnp.where(same, s + 1, found)
        found_entry = jnp.where(same, entry[:, s : s + 1], found_entry)
    used = found > 0

    def only(x):
        return jnp.sum(jnp.where(used, x, 0).astype(F32), axis=0, keepdims=True).astype(I32)

    any_used = only(found) > 0
    head = only(head_row)
    piece = only(piece)
    inner = (head - only(head_row // per * per)) * sessions + only(found) - 1
    size = per * sessions
    unused = devices * size
    slot_ref[0:1, :] = jnp.where(any_used, piece * size + inner, unused)
    slot_ref[1:2, :] = jnp.where(any_used, (piece ^ 2) * size + inner, unused)
    slot_ref[2:3, :] = jnp.where(any_used, (piece ^ 1) * size + inner, unused)
    slot_ref[3:4, :] = jnp.where(any_used, head, -1)
    slot_ref[4:5, :] = jnp.where(any_used, only(found_entry), devices * capacity)
    slot_ref[5:8, :] = jnp.zeros((3, padded), I32)

    total = jnp.zeros(act_ref.shape, F32)
    for step in range(steps):
        part = slice(step * chunk, (step + 1) * chunk)
        total += jnp.dot(rows[:, part].astype(BF16), w_ref[part, :], preferred_element_type=F32)
    gate = jax.nn.sigmoid(total)
    is_gate = me * cols >= 3 * heads * 128
    active = jnp.where(is_gate, gate, total * gate).astype(BF16)
    act_ref[...] = jnp.dot(place, active, preferred_element_type=F32).astype(BF16)


def project(pieces, w, send, heads, slots):
    devices = len(pieces)
    own = pieces[0].shape[0] - 1
    sessions = own * devices
    width, cols = w.shape
    steps = 8
    padded = (slots + 127) // 128 * 128
    return pl.pallas_call(
        functools.partial(project_kernel, devices, heads, slots, steps),
        out_shape=(
            jax.ShapeDtypeStruct((sessions, cols), BF16),
            jax.ShapeDtypeStruct((heads, sessions), I32),
            jax.ShapeDtypeStruct((8, padded), I32),
        ),
        in_specs=[VMEM] * (2 + devices),
        out_specs=(VMEM, VMEM, VMEM),
        scratch_shapes=[
            pltpu.VMEM((sessions, width), F32),
        ],
        compiler_params=pltpu.CompilerParams(
            vmem_limit_bytes=grant(w, *pieces, jax.ShapeDtypeStruct((sessions, width), F32))
        ),
        cost_estimate=pl.CostEstimate(
            flops=2 * sessions * width * cols, bytes_accessed=2 * width * cols, transcendentals=0
        ),
        name="project",
    )(send, w, *pieces)


def readout_kernel(devices, *refs):
    slot_ref, rate_ref, scale_ref, cache_ref = refs[:4]
    pieces = refs[4 : 4 + devices]
    read_ref, flat_ref, key_ref, value_ref, query, reads, *stage = refs[4 + devices :]
    sessions, cols = pieces[0].shape
    per = cols // 128
    slots = cache_ref.shape[0]
    for j in range(devices):
        block = fetch(pieces[j], stage)
        for b in range(per):
            base = (j * per + b) * sessions
            flat_ref[base : base + sessions, :] = block[:, b * 128 : (b + 1) * 128].astype(F32)
    base = devices * per * sessions
    flat_ref[base : base + 8, :] = jnp.zeros((8, 128), F32)

    @pl.loop(0, slots // 8)
    def _(group):
        for u in range(8):
            e = group * 8 + u
            query[pl.ds(e, 1), :] = flat_ref[pl.ds(slot_ref[0, e], 1), :]
            key_ref[pl.ds(e, 1), :] = flat_ref[pl.ds(slot_ref[1, e], 1), :]
            value_ref[pl.ds(e, 1), :] = flat_ref[pl.ds(slot_ref[2, e], 1), :]

    rows8 = lax.broadcasted_iota(I32, (8, 128), 0)
    for base in range(0, slots, 8):
        q8 = query[base : base + 8, :]
        decay, scale = factors(slot_ref, rate_ref, scale_ref, base)
        wide = jnp.concatenate([cache_ref[base + u] for u in range(8)], axis=1)
        prod = jnp.dot(q8.astype(BF16), wide, preferred_element_type=F32)
        seen = jnp.zeros((8, 128), F32)
        for u in range(8):
            seen = jnp.where(rows8 == u, prod[:, u * 128 : (u + 1) * 128], seen)
        near = jnp.sum(q8 * key_ref[base : base + 8, :], axis=1, keepdims=True)
        result = seen * (decay * scale) + near * value_ref[base : base + 8, :]
        for u in range(8):
            reads[pl.ds(slot_ref[4, base + u], 1), :] = result[u : u + 1, :]
    entries = read_ref.shape[0]
    read_ref[...] = reads[:entries, :].astype(BF16)


def factors(slot_ref, rate_ref, scale_ref, base):
    rows8 = lax.broadcasted_iota(I32, (8, 128), 0)
    rate = jnp.zeros((8, 128), F32)
    scale = jnp.ones((8, 128), F32)
    for u in range(8):
        head = slot_ref[3, base + u]
        one = jnp.where(head < 0, 0.0, rate_ref[jnp.maximum(head, 0)])
        rate = jnp.where(rows8 == u, one, rate)
        scale = jnp.where(rows8 == u, scale_ref[base + u], scale)
    return jnp.exp(-rate), scale


def read_states(pieces, cache, slot, rate, scale, capacity):
    devices = len(pieces)
    entries = devices * capacity
    sessions, cols = pieces[0].shape
    slots = cache.shape[0]
    large = is_large(*pieces)
    flat = jax.ShapeDtypeStruct((devices * sessions * cols // 128 + 8, 128), F32)
    rows = jax.ShapeDtypeStruct((slots, 128), F32)
    return pl.pallas_call(
        functools.partial(readout_kernel, devices),
        out_shape=(jax.ShapeDtypeStruct((entries, 128), BF16), flat, rows, rows),
        in_specs=[SMEM] * 3 + [VMEM] + [ANY if large else VMEM] * devices,
        out_specs=(VMEM, VMEM, VMEM, VMEM),
        scratch_shapes=[
            pltpu.VMEM((slots, 128), F32),
            pltpu.VMEM((entries + 8, 128), F32),
        ]
        + ([pltpu.VMEM((sessions, cols), BF16), pltpu.SemaphoreType.DMA] if large else []),
        compiler_params=pltpu.CompilerParams(
            vmem_limit_bytes=grant(cache, flat, *([] if large else pieces))
        ),
        cost_estimate=pl.CostEstimate(
            flops=2 * cache.size, bytes_accessed=8 * cache.size, transcendentals=0
        ),
        name="readout",
    )(slot, rate, scale, cache, *pieces)


def update_kernel(first, count, *refs):
    slot_ref, rate_ref, scale_ref, cache_ref, key_ref, value_ref = refs[:6]
    out_ref, fresh, sems = refs[-3:]
    rows8 = lax.broadcasted_iota(I32, (8, 128), 0)
    backs = []
    for base in range(first, first + count, 8):
        decay, scale = factors(slot_ref, rate_ref, scale_ref, base)
        scaled = value_ref[base : base + 8, :] * (1.0 / scale)
        high = scaled.astype(BF16).astype(F32)
        spread = jnp.concatenate(
            [
                jnp.concatenate([jnp.where(rows8 == u, term, 0.0) for u in range(8)], axis=1)
                for term in (high, scaled - high)
            ],
            axis=0,
        ).astype(BF16)
        columns = jnp.concatenate([key_ref[base : base + 8, :]] * 2, axis=0).T.astype(BF16)
        outer = jnp.dot(columns, spread, preferred_element_type=F32)
        for u in range(8):
            fresh[base - first + u] = (
                decay[u : u + 1, :] * cache_ref[base + u].astype(F32)
                + outer[:, u * 128 : (u + 1) * 128]
            ).astype(BF16)
        backs.append(
            pltpu.make_async_copy(
                fresh.at[pl.ds(base - first, 8)],
                out_ref.at[pl.ds(base, 8)],
                sems.at[(base - first) // 8],
            )
        )
        backs[-1].start()
    for back in backs:
        back.wait()


def update_tiles(cache, key_rows, values, slot, rate, scale, first, count, begun):
    return pl.pallas_call(
        functools.partial(update_kernel, first, count),
        out_shape=jax.ShapeDtypeStruct(cache.shape, BF16),
        in_specs=[SMEM] * 3 + [VMEM] * 3 + [ANY] * len(begun),
        out_specs=ANY,
        scratch_shapes=[
            pltpu.VMEM((count, 128, 128), BF16),
            pltpu.SemaphoreType.DMA((count // 8,)),
        ],
        input_output_aliases={6: 0} if begun else {},
        compiler_params=pltpu.CompilerParams(vmem_limit_bytes=grant(cache, cache)),
        cost_estimate=pl.CostEstimate(
            flops=0, bytes_accessed=4 * count * 128 * 128, transcendentals=0
        ),
        name="update",
    )(slot, rate, scale, cache, key_rows, values, *begun)


def finish_kernel(devices, per, *refs):
    pick_ref, act_ref, gain_ref, w_ref = refs[:4]
    pieces = refs[4 : 4 + devices]
    out_ref, flat, hidden, merged, *stages = refs[4 + devices :]
    entries = pieces[0].shape[0]
    sessions = merged.shape[0]
    heads = merged.shape[1] // 128
    me = lax.axis_index("batch")
    for j in range(devices):
        flat[j * entries : (j + 1) * entries, :] = fetch(pieces[j], stages[:2]).astype(F32)

    @pl.loop(0, heads)
    def _(h):
        base = pl.multiple_of(h * sessions, 8)
        for s in range(sessions):
            hidden[pl.ds(base + s, 1), :] = flat[pl.ds(pick_ref[h, s], 1), :]

    squares = jnp.zeros((sessions, 128), F32)
    for h in range(heads):
        block = hidden[h * sessions : (h + 1) * sessions, :]
        squares += block * block
    mean = jnp.sum(squares, axis=1, keepdims=True) * (1.0 / (heads * 128))
    norm = lax.rsqrt(mean + 1e-6)
    for h in range(heads):
        block = hidden[h * sessions : (h + 1) * sessions, :]
        piece = place_of(me ^ (3 * devices // 4 + h // per), devices)
        base = pl.multiple_of((piece * per + h % per) * sessions, 8)
        gate = fetch(act_ref.at[pl.ds(base, sessions)], stages[2:])
        block = block * norm * gain_ref[h : h + 1, :] * gate
        merged[:, h * 128 : (h + 1) * 128] = block.astype(BF16)
    out_ref[...] = jnp.dot(merged[...], w_ref[...], preferred_element_type=F32).astype(BF16)


def finish(pieces, gates, pick, gain, w_out):
    devices = len(pieces)
    entries = pieces[0].shape[0]
    heads, sessions = pick.shape
    per = gates.shape[0] // (devices * sessions)
    large = is_large(gates)
    width = w_out.shape[0]
    return pl.pallas_call(
        functools.partial(finish_kernel, devices, per),
        out_shape=jax.ShapeDtypeStruct((sessions, w_out.shape[1]), BF16),
        in_specs=[SMEM, ANY if large else VMEM, VMEM, VMEM] + [ANY if large else VMEM] * devices,
        out_specs=VMEM,
        scratch_shapes=[
            pltpu.VMEM((devices * entries, 128), F32),
            pltpu.VMEM((sessions * width // 128, 128), F32),
            pltpu.VMEM((sessions, width), BF16),
        ]
        + (
            [
                pltpu.VMEM((entries, 128), BF16),
                pltpu.SemaphoreType.DMA,
                pltpu.VMEM((sessions, 128), F32),
                pltpu.SemaphoreType.DMA,
            ]
            if large
            else []
        ),
        compiler_params=pltpu.CompilerParams(
            vmem_limit_bytes=grant(
                w_out,
                *([] if large else [gates, *pieces]),
                jax.ShapeDtypeStruct((devices * entries, 128), F32),
                jax.ShapeDtypeStruct((sessions * width // 128, 192), F32),
            )
        ),
        cost_estimate=pl.CostEstimate(
            flops=2 * sessions * w_out.size, bytes_accessed=2 * w_out.size, transcendentals=0
        ),
        name="finish",
    )(pick, gates, gain, w_out, *pieces)


def on_device(
    tokens,
    w_proj,
    w_out,
    decay_rate,
    norm_gain,
    cache_tiles,
    tile_scales,
    tile_holder,
    tile_rank,
    send_slot,
):
    devices = lax.axis_size("batch")
    heads = decay_rate.shape[0]
    capacity = send_slot.shape[-1]
    slots = cache_tiles.shape[0]

    sent = pack(tokens, tile_holder * capacity + tile_rank)
    high, low = devices // 2, devices // 4
    direct = [cross(sent, bit, devices) for bit in (high, low, high ^ low)]
    tokens_all = gather_pieces([sent] + direct, devices // 8, devices)
    act, pick, slot = project(
        tokens_all, w_proj, jnp.transpose(send_slot, (2, 0, 1)), heads, slots
    )
    act_all = gather_pieces([act], devices // 2, devices)
    read, gates, key_rows, values = read_states(
        act_all, cache_tiles, slot, decay_rate, tile_scales, capacity
    )
    half = slots // 16 * 8
    update = functools.partial(
        update_tiles, cache_tiles, key_rows, values, slot, decay_rate, tile_scales
    )
    high, low = devices // 2, devices // 4
    bits = [1 << k for k in reversed(range(1, devices.bit_length() - 3))]
    first = [cross(read, bit, devices) for bit in (high, low, high ^ low, *bits)]
    new_cache = update(0, half, [])
    *first, new_cache = lax.optimization_barrier((*first, new_cache))
    held = [read] + first[:3]
    for own_piece, bit in zip(first[3:], bits):
        last = [cross(piece, bit, devices) for piece in held[1:]]
        held = held + [own_piece] + last
    early = [cross(piece, 1, devices) for piece in held[: len(held) - len(last)]]
    *early, new_cache = lax.optimization_barrier((*early, new_cache))
    new_cache = update(half, slots - half, [new_cache])
    *last, new_cache = lax.optimization_barrier((*last, new_cache))
    held = held[: len(held) - len(last)] + last
    read_all = held + early + [cross(piece, 1, devices) for piece in last]
    mixed_out = finish(read_all, gates, pick, norm_gain.reshape(heads, 128), w_out)
    return (mixed_out, new_cache)


def solution(mesh):
    return jax.shard_map(
        on_device,
        mesh=mesh,
        in_specs=(
            P(("groups", "batch"), None),
            P(None, "batch"),
            P(None, "batch"),
            P(),
            P(),
            P(("groups", "batch"), None, None),
            P(("groups", "batch")),
            P(("groups", "batch"), None),
            P(("groups", "batch"), None),
            P(("groups", "batch"), None, None),
        ),
        out_specs=(P("groups", "batch"), P(("groups", "batch"), None, None)),
        check_vma=False,
    )
```

```python
import functools
import math

import jax
import jax.numpy as jnp
from jax import lax
from jax.experimental import pallas as pl
from jax.experimental.pallas import tpu as pltpu
from jax.sharding import PartitionSpec as P

BF16 = jnp.bfloat16
F32 = jnp.float32
I32 = jnp.int32
SMEM = pl.BlockSpec(memory_space=pltpu.SMEM)
VMEM = pl.BlockSpec(memory_space=pltpu.VMEM)
ANY = pl.BlockSpec(memory_space=pl.ANY)


def grant(*arrays):
    held = sum(math.prod(a.shape) * jnp.dtype(a.dtype).itemsize for a in arrays)
    most = 60 * 1024 * 1024
    return held + 6 * 1024 * 1024 if held < most // 2 else most


def block_order(devices):
    order, bit = [0], devices // 2
    while bit >= 1:
        order = order + [o ^ bit for o in order]
        bit //= 2
    return order


def place_of(crossed, devices):
    bits = devices.bit_length() - 1
    return sum(((crossed >> k) & 1) << (bits - 1 - k) for k in range(bits))


def cross(piece, bit, devices):
    return lax.ppermute(piece, "batch", [(i, i ^ bit) for i in range(devices)])


def gather_pieces(held, bit, devices):
    while bit >= 1:
        held = held + [cross(piece, bit, devices) for piece in held]
        bit //= 2
    return held


def is_large(*arrays):
    return sum(math.prod(a.shape) * jnp.dtype(a.dtype).itemsize for a in arrays) > 6 * 1024 * 1024


def fetch(ref, stage):
    if not stage:
        return ref[...]
    copy = pltpu.make_async_copy(ref, *stage)
    copy.start()
    copy.wait()
    return stage[0][...]


def pack_kernel(tokens_ref, origin_ref, out_ref):
    own, width = tokens_ref.shape
    heads = origin_ref.shape[1]
    parts = []
    for i in range(own):
        parts.append(origin_ref[i : i + 1, :].astype(F32))
        parts.append(jnp.zeros((1, 128 - heads), F32))
    parts.append(jnp.zeros((1, width - own * 128), F32))
    table = jnp.concatenate(parts, axis=1)
    block = jnp.concatenate([tokens_ref[...].astype(F32), table], axis=0)
    out_ref[...] = block.astype(BF16)


def pack(tokens, origin):
    own, width = tokens.shape
    return pl.pallas_call(
        pack_kernel,
        out_shape=jax.ShapeDtypeStruct((own + 1, width), BF16),
        in_specs=[VMEM] * 2,
        out_specs=VMEM,
        compiler_params=pltpu.CompilerParams(vmem_limit_bytes=grant(tokens)),
        cost_estimate=pl.CostEstimate(flops=20000000000, bytes_accessed=60000000, transcendentals=0),
        name="pack",
    )(tokens, origin)


def project_kernel(devices, heads, slots, steps, *refs):
    send_ref, w_ref = refs[:2]
    pieces = refs[2 : 2 + devices]
    act_ref, pick_ref, slot_ref, rows = refs[2 + devices :]
    order = block_order(devices)
    sessions, cols = act_ref.shape
    per = cols // 128
    own = sessions // devices
    capacity = send_ref.shape[0]
    width = w_ref.shape[0]
    chunk = width // steps
    me = lax.axis_index("batch")
    lane = lax.broadcasted_iota(I32, (1, sessions), 1)
    target = jnp.zeros((1, sessions), I32)
    source = jnp.zeros((1, sessions), I32)
    indices = []
    for j in range(devices):
        block = pieces[j][...].astype(F32)
        rows[j * own : (j + 1) * own, :] = block[:own]
        for i in range(own):
            indices.append(block[own : own + 1, i * 128 : (i + 1) * 128])
        inside = (lane >= j * own) & (lane < (j + 1) * own)
        target = jnp.where(inside, lane + ((me ^ order[j]) - j) * own, target)
        source = jnp.where(inside, lane + (place_of(me ^ j, devices) - j) * own, source)
    grid_row = lax.broadcasted_iota(I32, (sessions, sessions), 0)
    place = (grid_row == target).astype(F32).astype(BF16)
    place_t = (grid_row == source).astype(F32).astype(BF16)

    table = jnp.concatenate(indices, axis=0)
    table = jnp.dot(table.T.astype(BF16), place_t, preferred_element_type=F32).astype(I32)
    origin = table[:heads]
    holder = (origin * (65536 // capacity + 1)) >> 16
    rank = origin - holder * capacity
    owner = (lane * (65536 // own + 1)) >> 16
    pick_ref[...] = (place_of(holder ^ me, devices) * devices + owner) * capacity + rank

    owner_row = lax.broadcasted_iota(I32, (devices, sessions), 0)
    spread = (owner_row == owner).astype(F32).astype(BF16)
    sent = jnp.concatenate([send_ref[r].astype(F32) for r in range(capacity)], axis=0).astype(BF16)
    sent = jnp.dot(sent, spread, preferred_element_type=F32).astype(I32)
    slot = jnp.full((heads, sessions), -1, I32)
    for r in range(capacity):
        slot = jnp.where(rank == r, sent[r : r + 1, :], slot)
    slot = jnp.where(holder == me, slot, -1)
    entry = owner * capacity + rank
    padded = slot_ref.shape[1]
    slot_lane = lax.broadcasted_iota(I32, (heads, padded), 1)
    head_row = lax.broadcasted_iota(I32, (heads, padded), 0)
    piece = jnp.zeros((heads, padded), I32)
    for group in range(heads // per):
        inside = (head_row >= group * per) & (head_row < (group + 1) * per)
        piece = jnp.where(inside, place_of(me ^ group, devices), piece)
    found = jnp.zeros((heads, padded), I32)
    found_entry = jnp.zeros((heads, padded), I32)
    for s in range(sessions):
        same = slot[:, s : s + 1] == slot_lane
        found = jnp.where(same, s + 1, found)
        found_entry = jnp.where(same, entry[:, s : s + 1], found_entry)
    used = found > 0

    def only(x):
        return jnp.sum(jnp.where(used, x, 0).astype(F32), axis=0, keepdims=True).astype(I32)

    any_used = only(found) > 0
    head = only(head_row)
    piece = only(piece)
    inner = (head - only(head_row // per * per)) * sessions + only(found) - 1
    size = per * sessions
    unused = devices * size
    slot_ref[0:1, :] = jnp.where(any_used, piece * size + inner, unused)
    slot_ref[1:2, :] = jnp.where(any_used, (piece ^ 2) * size + inner, unused)
    slot_ref[2:3, :] = jnp.where(any_used, (piece ^ 1) * size + inner, unused)
    slot_ref[3:4, :] = jnp.where(any_used, head, -1)
    slot_ref[4:5, :] = jnp.where(any_used, only(found_entry), devices * capacity)
    slot_ref[5:8, :] = jnp.zeros((3, padded), I32)

    total = jnp.zeros(act_ref.shape, F32)
    for step in range(steps):
        part = slice(step * chunk, (step + 1) * chunk)
        total += jnp.dot(rows[:, part].astype(BF16), w_ref[part, :], preferred_element_type=F32)
    gate = jax.nn.sigmoid(total)
    is_gate = me * cols >= 3 * heads * 128
    active = jnp.where(is_gate, gate, total * gate).astype(BF16)
    act_ref[...] = jnp.dot(place, active, preferred_element_type=F32).astype(BF16)


def project(pieces, w, send, heads, slots):
    devices = len(pieces)
    own = pieces[0].shape[0] - 1
    sessions = own * devices
    width, cols = w.shape
    steps = 8
    padded = (slots + 127) // 128 * 128
    return pl.pallas_call(
        functools.partial(project_kernel, devices, heads, slots, steps),
        out_shape=(
            jax.ShapeDtypeStruct((sessions, cols), BF16),
            jax.ShapeDtypeStruct((heads, sessions), I32),
            jax.ShapeDtypeStruct((8, padded), I32),
        ),
        in_specs=[VMEM] * (2 + devices),
        out_specs=(VMEM, VMEM, VMEM),
        scratch_shapes=[
            pltpu.VMEM((sessions, width), F32),
        ],
        compiler_params=pltpu.CompilerParams(
            vmem_limit_bytes=grant(w, *pieces, jax.ShapeDtypeStruct((sessions, width), F32))
        ),
        cost_estimate=pl.CostEstimate(
            flops=2 * sessions * width * cols, bytes_accessed=2 * width * cols, transcendentals=0
        ),
        name="project",
    )(send, w, *pieces)


def readout_kernel(devices, *refs):
    slot_ref, rate_ref, scale_ref, cache_ref = refs[:4]
    pieces = refs[4 : 4 + devices]
    read_ref, flat_ref, key_ref, value_ref, query, reads, *stage = refs[4 + devices :]
    sessions, cols = pieces[0].shape
    per = cols // 128
    slots = cache_ref.shape[0]
    for j in range(devices):
        block = fetch(pieces[j], stage)
        for b in range(per):
            base = (j * per + b) * sessions
            flat_ref[base : base + sessions, :] = block[:, b * 128 : (b + 1) * 128].astype(F32)
    base = devices * per * sessions
    flat_ref[base : base + 8, :] = jnp.zeros((8, 128), F32)

    @pl.loop(0, slots // 8)
    def _(group):
        for u in range(8):
            e = group * 8 + u
            query[pl.ds(e, 1), :] = flat_ref[pl.ds(slot_ref[0, e], 1), :]
            key_ref[pl.ds(e, 1), :] = flat_ref[pl.ds(slot_ref[1, e], 1), :]
            value_ref[pl.ds(e, 1), :] = flat_ref[pl.ds(slot_ref[2, e], 1), :]

    rows8 = lax.broadcasted_iota(I32, (8, 128), 0)
    for base in range(0, slots, 8):
        q8 = query[base : base + 8, :]
        decay, scale = factors(slot_ref, rate_ref, scale_ref, base)
        wide = jnp.concatenate([cache_ref[base + u] for u in range(8)], axis=1)
        prod = jnp.dot(q8.astype(BF16), wide, preferred_element_type=F32)
        seen = jnp.zeros((8, 128), F32)
        for u in range(8):
            seen = jnp.where(rows8 == u, prod[:, u * 128 : (u + 1) * 128], seen)
        near = jnp.sum(q8 * key_ref[base : base + 8, :], axis=1, keepdims=True)
        result = seen * (decay * scale) + near * value_ref[base : base + 8, :]
        for u in range(8):
            reads[pl.ds(slot_ref[4, base + u], 1), :] = result[u : u + 1, :]
    entries = read_ref.shape[0]
    read_ref[...] = reads[:entries, :].astype(BF16)


def factors(slot_ref, rate_ref, scale_ref, base):
    rows8 = lax.broadcasted_iota(I32, (8, 128), 0)
    rate = jnp.zeros((8, 128), F32)
    scale = jnp.ones((8, 128), F32)
    for u in range(8):
        head = slot_ref[3, base + u]
        one = jnp.where(head < 0, 0.0, rate_ref[jnp.maximum(head, 0)])
        rate = jnp.where(rows8 == u, one, rate)
        scale = jnp.where(rows8 == u, scale_ref[base + u], scale)
    return jnp.exp(-rate), scale


def read_states(pieces, cache, slot, rate, scale, capacity):
    devices = len(pieces)
    entries = devices * capacity
    sessions, cols = pieces[0].shape
    slots = cache.shape[0]
    large = is_large(*pieces)
    flat = jax.ShapeDtypeStruct((devices * sessions * cols // 128 + 8, 128), F32)
    rows = jax.ShapeDtypeStruct((slots, 128), F32)
    return pl.pallas_call(
        functools.partial(readout_kernel, devices),
        out_shape=(jax.ShapeDtypeStruct((entries, 128), BF16), flat, rows, rows),
        in_specs=[SMEM] * 3 + [VMEM] + [ANY if large else VMEM] * devices,
        out_specs=(VMEM, VMEM, VMEM, VMEM),
        scratch_shapes=[
            pltpu.VMEM((slots, 128), F32),
            pltpu.VMEM((entries + 8, 128), F32),
        ]
        + ([pltpu.VMEM((sessions, cols), BF16), pltpu.SemaphoreType.DMA] if large else []),
        compiler_params=pltpu.CompilerParams(
            vmem_limit_bytes=grant(cache, flat, *([] if large else pieces))
        ),
        cost_estimate=pl.CostEstimate(
            flops=2 * cache.size, bytes_accessed=8 * cache.size, transcendentals=0
        ),
        name="readout",
    )(slot, rate, scale, cache, *pieces)


def update_kernel(first, count, *refs):
    slot_ref, rate_ref, scale_ref, cache_ref, key_ref, value_ref = refs[:6]
    out_ref, fresh, sems = refs[-3:]
    rows8 = lax.broadcasted_iota(I32, (8, 128), 0)
    backs = []
    for base in range(first, first + count, 8):
        decay, scale = factors(slot_ref, rate_ref, scale_ref, base)
        scaled = value_ref[base : base + 8, :] * (1.0 / scale)
        high = scaled.astype(BF16).astype(F32)
        spread = jnp.concatenate(
            [
                jnp.concatenate([jnp.where(rows8 == u, term, 0.0) for u in range(8)], axis=1)
                for term in (high, scaled - high)
            ],
            axis=0,
        ).astype(BF16)
        columns = jnp.concatenate([key_ref[base : base + 8, :]] * 2, axis=0).T.astype(BF16)
        outer = jnp.dot(columns, spread, preferred_element_type=F32)
        for u in range(8):
            fresh[base - first + u] = (
                decay[u : u + 1, :] * cache_ref[base + u].astype(F32)
                + outer[:, u * 128 : (u + 1) * 128]
            ).astype(BF16)
        backs.append(
            pltpu.make_async_copy(
                fresh.at[pl.ds(base - first, 8)],
                out_ref.at[pl.ds(base, 8)],
                sems.at[(base - first) // 8],
            )
        )
        backs[-1].start()
    for back in backs:
        back.wait()


def update_tiles(cache, key_rows, values, slot, rate, scale, first, count, begun):
    return pl.pallas_call(
        functools.partial(update_kernel, first, count),
        out_shape=jax.ShapeDtypeStruct(cache.shape, BF16),
        in_specs=[SMEM] * 3 + [VMEM] * 3 + [ANY] * len(begun),
        out_specs=ANY,
        scratch_shapes=[
            pltpu.VMEM((count, 128, 128), BF16),
            pltpu.SemaphoreType.DMA((count // 8,)),
        ],
        input_output_aliases={6: 0} if begun else {},
        compiler_params=pltpu.CompilerParams(vmem_limit_bytes=grant(cache, cache)),
        cost_estimate=pl.CostEstimate(
            flops=0, bytes_accessed=4 * count * 128 * 128, transcendentals=0
        ),
        name="update",
    )(slot, rate, scale, cache, key_rows, values, *begun)


def finish_kernel(devices, per, *refs):
    pick_ref, act_ref, gain_ref, w_ref = refs[:4]
    pieces = refs[4 : 4 + devices]
    out_ref, flat, hidden, merged, *stages = refs[4 + devices :]
    entries = pieces[0].shape[0]
    sessions = merged.shape[0]
    heads = merged.shape[1] // 128
    me = lax.axis_index("batch")
    for j in range(devices):
        flat[j * entries : (j + 1) * entries, :] = fetch(pieces[j], stages[:2]).astype(F32)

    @pl.loop(0, heads, unroll=4)
    def _(h):
        base = pl.multiple_of(h * sessions, 8)
        for s in range(sessions):
            hidden[pl.ds(base + s, 1), :] = flat[pl.ds(pick_ref[h, s], 1), :]

    squares = jnp.zeros((sessions, 128), F32)
    for h in range(heads):
        block = hidden[h * sessions : (h + 1) * sessions, :]
        squares += block * block
    mean = jnp.sum(squares, axis=1, keepdims=True) * (1.0 / (heads * 128))
    norm = lax.rsqrt(mean + 1e-6)
    for h in range(heads):
        block = hidden[h * sessions : (h + 1) * sessions, :]
        piece = place_of(me ^ (3 * devices // 4 + h // per), devices)
        base = pl.multiple_of((piece * per + h % per) * sessions, 8)
        gate = fetch(act_ref.at[pl.ds(base, sessions)], stages[2:])
        block = block * norm * gain_ref[h : h + 1, :] * gate
        merged[:, h * 128 : (h + 1) * 128] = block.astype(BF16)
    out_ref[...] = jnp.dot(merged[...], w_ref[...], preferred_element_type=F32).astype(BF16)


def finish(pieces, gates, pick, gain, w_out):
    devices = len(pieces)
    entries = pieces[0].shape[0]
    heads, sessions = pick.shape
    per = gates.shape[0] // (devices * sessions)
    large = is_large(gates)
    width = w_out.shape[0]
    return pl.pallas_call(
        functools.partial(finish_kernel, devices, per),
        out_shape=jax.ShapeDtypeStruct((sessions, w_out.shape[1]), BF16),
        in_specs=[SMEM, ANY if large else VMEM, VMEM, VMEM] + [ANY if large else VMEM] * devices,
        out_specs=VMEM,
        scratch_shapes=[
            pltpu.VMEM((devices * entries, 128), F32),
            pltpu.VMEM((sessions * width // 128, 128), F32),
            pltpu.VMEM((sessions, width), BF16),
        ]
        + (
            [
                pltpu.VMEM((entries, 128), BF16),
                pltpu.SemaphoreType.DMA,
                pltpu.VMEM((sessions, 128), F32),
                pltpu.SemaphoreType.DMA,
            ]
            if large
            else []
        ),
        compiler_params=pltpu.CompilerParams(
            vmem_limit_bytes=grant(
                w_out,
                *([] if large else [gates, *pieces]),
                jax.ShapeDtypeStruct((devices * entries, 128), F32),
                jax.ShapeDtypeStruct((sessions * width // 128, 192), F32),
            )
        ),
        cost_estimate=pl.CostEstimate(
            flops=2 * sessions * w_out.size, bytes_accessed=2 * w_out.size, transcendentals=0
        ),
        name="finish",
    )(pick, gates, gain, w_out, *pieces)


def on_device(
    tokens,
    w_proj,
    w_out,
    decay_rate,
    norm_gain,
    cache_tiles,
    tile_scales,
    tile_holder,
    tile_rank,
    send_slot,
):
    devices = lax.axis_size("batch")
    heads = decay_rate.shape[0]
    capacity = send_slot.shape[-1]
    slots = cache_tiles.shape[0]

    sent = pack(tokens, tile_holder * capacity + tile_rank)
    high, low = devices // 2, devices // 4
    direct = [cross(sent, bit, devices) for bit in (high, low, high ^ low)]
    tokens_all = gather_pieces([sent] + direct, devices // 8, devices)
    act, pick, slot = project(
        tokens_all, w_proj, jnp.transpose(send_slot, (2, 0, 1)), heads, slots
    )
    act_all = gather_pieces([act], devices // 2, devices)
    read, gates, key_rows, values = read_states(
        act_all, cache_tiles, slot, decay_rate, tile_scales, capacity
    )
    half = slots // 16 * 8
    update = functools.partial(
        update_tiles, cache_tiles, key_rows, values, slot, decay_rate, tile_scales
    )
    high, low = devices // 2, devices // 4
    bits = [1 << k for k in reversed(range(1, devices.bit_length() - 3))]
    first = [cross(read, bit, devices) for bit in (high, low, high ^ low, *bits)]
    new_cache = update(0, half, [])
    *first, new_cache = lax.optimization_barrier((*first, new_cache))
    held = [read] + first[:3]
    for own_piece, bit in zip(first[3:], bits):
        last = [cross(piece, bit, devices) for piece in held[1:]]
        held = held + [own_piece] + last
    early = [cross(piece, 1, devices) for piece in held[: len(held) - len(last)]]
    *early, new_cache = lax.optimization_barrier((*early, new_cache))
    new_cache = update(half, slots - half, [new_cache])
    *last, new_cache = lax.optimization_barrier((*last, new_cache))
    held = held[: len(held) - len(last)] + last
    read_all = held + early + [cross(piece, 1, devices) for piece in last]
    mixed_out = finish(read_all, gates, pick, norm_gain.reshape(heads, 128), w_out)
    return (mixed_out, new_cache)


def solution(mesh):
    return jax.shard_map(
        on_device,
        mesh=mesh,
        in_specs=(
            P(("groups", "batch"), None),
            P(None, "batch"),
            P(None, "batch"),
            P(),
            P(),
            P(("groups", "batch"), None, None),
            P(("groups", "batch")),
            P(("groups", "batch"), None),
            P(("groups", "batch"), None),
            P(("groups", "batch"), None, None),
        ),
        out_specs=(P("groups", "batch"), P(("groups", "batch"), None, None)),
        check_vma=False,
    )
```
